256 devices in a mesh: fsdp: 64 (over z, x, y_hi), tp: 4 (over y_lo, core).
Axes of the slice: x: 4, y: 4 (y_hi: 2, y_lo: 2; y = y_hi * 2 + y_lo), z: 8, core: 2. Of those that a mesh axis runs over, the one named last changes fastest.
Arguments:
- tokens: bfloat16 [256, 8192], P('fsdp', 'tp'), may hold values from -6 to 6
- token_adapter_index: int32 [256], replicated, may hold values from 0 to 3
- gate_projection_weight: bfloat16 [8192, 16384], P('tp', 'fsdp'), may hold values from -0.0625 to 0.0625
- up_projection_weight: bfloat16 [8192, 16384], P('tp', 'fsdp'), may hold values from -0.0625 to 0.0625
- down_projection_weight: bfloat16 [16384, 8192], P('fsdp', 'tp'), may hold values from -0.046875 to 0.046875
- adapter_input_maps: bfloat16 [4, 64, 8192], P(None, None, 'tp'), may hold values from -0.0625 to 0.0625
- adapter_output_maps: bfloat16 [4, 64, 16384], P(None, None, 'fsdp'), may hold values from -0.75 to 0.75
- cotangent: bfloat16 [256, 8192], P('fsdp', 'tp'), may hold values from -6 to 6
Outputs:
- reference_out: bfloat16 [256, 8192], P('fsdp', 'tp')
- policy_out: bfloat16 [256, 8192], P('fsdp', 'tp')
- input_map_gradient: float32 [4, 64, 8192], P(None, None, 'tp')
- output_map_gradient: float32 [4, 64, 16384], P(None, None, 'fsdp')
The draws below stay inside these ranges and needn't reach their ends.
All inputs are finite; a program needn't handle non-finite values.
Results may differ from the reference program's by a relative error of at most 0.015.
Values may be sent and summed in bfloat16 or wider, within the bound.
A program may use at most 64 MiB of HBM per device.

```python
import jax
import jax.numpy as jnp

MODEL_WIDTH = 8192
HIDDEN_UNITS = 16384
ADAPTER_RANK = 64
ADAPTER_COUNT = 4
TOKENS = 256


def set_ends(array, own_key, low, high):
    longest = array.shape.index(max(array.shape))
    spots = []
    for shift in (0, 1):
        where = [jax.random.randint(jax.random.fold_in(own_key, axis), (), 0, length) for axis, length in enumerate(array.shape)]
        where[longest] = (where[longest] + shift) % array.shape[longest]
        spots.append(tuple(where))
    return array.at[spots[0]].set(low).at[spots[1]].set(high)


def shard_levels(key, dims, cuts, smallest, top_value):
    factor_of = 1.0
    for dim, blocks in cuts:
        draws = jax.random.uniform(jax.random.fold_in(jax.random.fold_in(key, 6), dim), (blocks,), jnp.float32, smallest / len(cuts), top_value / len(cuts))
        factor_of = factor_of * jnp.repeat(jnp.exp(draws), dims[dim] // blocks).reshape((-1,) + (1,) * (len(dims) - 1 - dim))
    return factor_of


def normal_values(own_key, extent, spread, bound, pieces=(), kind=jnp.bfloat16):
    loudness = shard_levels(own_key, extent, pieces, -0.22, 0.18) if pieces else 1.0
    array = jax.random.normal(own_key, extent, jnp.float32) * spread * loudness
    return jnp.minimum(jnp.maximum(array, -bound), bound).astype(kind)


def setup_inputs(seed: int = 0) -> dict:
    keys = jax.random.split(jax.random.key(seed), 9)
    tokens = normal_values(keys[0], (TOKENS, MODEL_WIDTH), 1.0, 6.0, ((0, 64), (1, 4)))
    token_adapter_index = set_ends(jax.random.randint(keys[1], (TOKENS,), 0, ADAPTER_COUNT), jax.random.fold_in(keys[1], 1), 0, ADAPTER_COUNT - 1).astype(jnp.int32)
    gate_projection_weight = normal_values(keys[2], (MODEL_WIDTH, HIDDEN_UNITS), MODEL_WIDTH ** -0.5, 0.0625, ((0, 4), (1, 64)))
    up_projection_weight = normal_values(keys[3], (MODEL_WIDTH, HIDDEN_UNITS), MODEL_WIDTH ** -0.5, 0.0625, ((0, 4), (1, 64)))
    down_projection_weight = normal_values(keys[4], (HIDDEN_UNITS, MODEL_WIDTH), HIDDEN_UNITS ** -0.5, 0.046875, ((0, 64), (1, 4)))
    adapter_input_maps = normal_values(keys[5], (ADAPTER_COUNT, ADAPTER_RANK, MODEL_WIDTH), MODEL_WIDTH ** -0.5, 0.0625, ((2, 4),))
    adapter_output_maps = normal_values(keys[6], (ADAPTER_COUNT, ADAPTER_RANK, HIDDEN_UNITS), ADAPTER_RANK ** -0.5, 0.75, ((2, 64),))
    cotangent = normal_values(keys[7], (TOKENS, MODEL_WIDTH), 1.0, 6.0, ((0, 64), (1, 4)))
    return {"tokens": tokens, "token_adapter_index": token_adapter_index, "gate_projection_weight": gate_projection_weight, "up_projection_weight": up_projection_weight, "down_projection_weight": down_projection_weight, "adapter_input_maps": adapter_input_maps, "adapter_output_maps": adapter_output_maps, "cotangent": cotangent}


def widen_rank(values, adapter_indicator):
    count = values.shape[0]
    return (adapter_indicator[:, :, None] * values[:, None, :].astype(jnp.float32)).reshape(count, -1).astype(jnp.bfloat16)


def adapter_selection(wide, adapter_indicator):
    count = wide.shape[0]
    return jnp.einsum("mj,mjr->mr", adapter_indicator, wide.reshape(count, adapter_indicator.shape[1], -1))


def reference(tokens, token_adapter_index, gate_projection_weight, up_projection_weight, down_projection_weight, adapter_input_maps, adapter_output_maps, cotangent):
    adapter_indicator = (token_adapter_index[:, None] == jnp.arange(ADAPTER_COUNT, dtype=jnp.int32)[None, :]).astype(jnp.float32)
    gate_values = jnp.dot(tokens, gate_projection_weight, preferred_element_type=jnp.float32)
    up_values = jnp.dot(tokens, up_projection_weight, preferred_element_type=jnp.float32)
    stacked_input_maps = adapter_input_maps.reshape(ADAPTER_COUNT * ADAPTER_RANK, MODEL_WIDTH)
    stacked_output_maps = adapter_output_maps.reshape(ADAPTER_COUNT * ADAPTER_RANK, HIDDEN_UNITS)
    adapter_total_sum = adapter_selection(jnp.dot(tokens, stacked_input_maps.T, preferred_element_type=jnp.float32), adapter_indicator)
    adapter_widened = widen_rank(adapter_total_sum.astype(jnp.bfloat16), adapter_indicator)
    activated = jax.nn.silu(gate_values)
    up_policy_values = up_values + jnp.dot(adapter_widened, stacked_output_maps, preferred_element_type=jnp.float32)
    hidden_ref = (activated * up_values).astype(jnp.bfloat16)
    hidden_pol = (activated * up_policy_values).astype(jnp.bfloat16)
    reference_out = jnp.dot(hidden_ref, down_projection_weight, preferred_element_type=jnp.float32).astype(jnp.bfloat16)
    policy_out = jnp.dot(hidden_pol, down_projection_weight, preferred_element_type=jnp.float32).astype(jnp.bfloat16)
    grad_hidden = jnp.dot(cotangent, down_projection_weight.T, preferred_element_type=jnp.float32)
    up_gradient = (grad_hidden * activated).astype(jnp.bfloat16)
    output_map_gradient = jnp.dot(adapter_widened.T, up_gradient, preferred_element_type=jnp.float32).reshape(ADAPTER_COUNT, ADAPTER_RANK, HIDDEN_UNITS)
    adapter_backward = adapter_selection(jnp.dot(up_gradient, stacked_output_maps.T, preferred_element_type=jnp.float32), adapter_indicator)
    backward_widened = widen_rank(adapter_backward.astype(jnp.bfloat16), adapter_indicator)
    input_map_gradient = jnp.dot(backward_widened.T, tokens, preferred_element_type=jnp.float32).reshape(ADAPTER_COUNT, ADAPTER_RANK, MODEL_WIDTH)
    return reference_out, policy_out, input_map_gradient, output_map_gradient
```

```python
import functools

import jax
import jax.numpy as jnp
from jax import lax
from jax.experimental import pallas as pl
from jax.experimental.pallas import tpu as pltpu
from jax.sharding import PartitionSpec as P

MESH = pl.DeviceIdType.MESH
BF = jnp.bfloat16
F32 = jnp.float32

GROUPS = (("z", 0, 512), ("p", 512, 768), ("p", 1280, 768))


def nt(a, b):
    return lax.dot_general(a, b, (((1,), (1,)), ((), ())), preferred_element_type=F32)


def tn(a, b):
    return lax.dot_general(a, b, (((0,), (0,)), ((), ())), preferred_element_type=F32)


def nn(a, b):
    return jnp.dot(a, b, preferred_element_type=F32)


def iota2(n, m):
    return (
        lax.broadcasted_iota(jnp.int32, (n, m), 0),
        lax.broadcasted_iota(jnp.int32, (n, m), 1),
    )


def as_matrix(condition):
    return condition.astype(F32).astype(BF)


def kernel(
    idx, tok, cot, gate, up, down, imaps, omaps,
    ref_out, pol_out, in_grad, out_grad,
    gate_v, up_v, down_v, imaps_v, omaps_v,
    ta, tb, ca, cb, xt, ct,
    f1, s1, r1, s2, r2, e1, er1,
    f2, g1, gr1, g2, gr2, e2, er2,
    act_v, mask_v, lw_v, href, hpol, gup, hrp, hpp,
    ar0, ar1, ar1s, ar2, ar2s, ar3,
    in_v, out_v,
    *rest,
):
    ngroups = len(GROUPS)
    ysend, yrecv, zsend, zrecv = (rest[i * ngroups : (i + 1) * ngroups] for i in range(4))
    wsem, ssem, rsem, osem = rest[4 * ngroups :]

    f = lax.axis_index("fsdp")
    t = lax.axis_index("tp")
    z, p, x, h, c = f // 8, f % 8, (f // 2) % 4, f % 2, t % 2

    def zdev(k):
        return {"fsdp": lax.rem(z + k + 8, 8) * 8 + p, "tp": t}

    def pidx(k):
        return lax.rem(x + k // 2, 4) * 2 + (h + k % 2) % 2

    def pdev(k):
        return {"fsdp": z * 8 + pidx(k), "tp": t}

    def tdev(k):
        return {"fsdp": f, "tp": ((t // 2 + k // 2) % 2) * 2 + (c + k % 2) % 2}

    counter = [0]
    pending = []

    def send(src, dst, device):
        n = counter[0]
        counter[0] += 1
        copy = pltpu.make_async_remote_copy(
            src_ref=src, dst_ref=dst, send_sem=ssem.at[n], recv_sem=rsem.at[n],
            device_id=device, device_id_type=MESH,
        )
        copy.start()
        pending.append(copy)
        return copy

    loads = []
    for n, (src, dst) in enumerate(
        ((gate, gate_v), (up, up_v), (imaps, imaps_v), (omaps, omaps_v), (down, down_v))
    ):
        load = pltpu.make_async_copy(src, dst, wsem.at[n])
        load.start()
        loads.append(load)

    barrier = pltpu.get_barrier_semaphore()
    partners = [zdev(k) for k in range(1, 8)] + [pdev(k) for k in range(1, 8)] + [tdev(k) for k in range(1, 4)]
    for device in partners:
        pl.semaphore_signal(barrier, 1, device_id=device, device_id_type=MESH)

    i16, j4 = iota2(16, 4)
    for src, half_a, half_b in ((tok, ta, tb), (cot, ca, cb)):
        packed = None
        for q in range(4):
            spread = as_matrix(i16 == q * 4 + j4)
            term = nn(spread, src[:, q * 512 : (q + 1) * 512])
            packed = term if packed is None else packed + term
        packed = packed.astype(BF)
        half_a[z, p] = packed[:, :256]
        half_b[z, p] = packed[:, 256:]

    i8, j8 = iota2(8, 256)
    chosen = as_matrix(idx[...] == i8)
    mask_v[...] = tn(chosen, as_matrix(i8 == j8 // 64)).astype(BF)

    pl.semaphore_wait(barrier, len(partners))

    def first_hops(half_a, half_b):
        a = [send(half_a.at[z, p], half_a.at[z, p], pdev(k)) for k in range(1, 8)]
        b = [send(half_b.at[z, p], half_b.at[z, p], zdev(k)) for k in range(1, 8)]
        return a, b

    def second_hops(half_a, half_b, first):
        a, b = first
        for copy in a:
            copy.wait_recv()
        near = [send(half_a.at[z], half_a.at[z], zdev(k)) for k in (2, -2, 1, -1)]
        for copy in b:
            copy.wait_recv()
        plane = [send(half_b.at[:, p], half_b.at[:, p], pdev(k)) for k in range(1, 8)]
        return near, plane

    def third_hops(half_a, second):
        near, _ = second
        far = []
        for n, sign in ((0, 1), (1, -1)):
            near[n].wait_recv()
            block = lax.rem(z - 2 * sign + 8, 8)
            part = half_a.at[block, pl.ds(0 if sign == 1 else 4, 4)]
            far.append(send(part, part, zdev(2 * sign)))
            far.append(send(half_a.at[block], half_a.at[block], zdev(sign)))
        return far

    def finish(second, far):
        near, plane = second
        for copy in near[2:] + plane + far:
            copy.wait_recv()

    first_t = first_hops(ta, tb)
    first_c = first_hops(ca, cb)
    second_t = second_hops(ta, tb, first_t)
    far_t = third_hops(ta, second_t)
    second_c = second_hops(ca, cb, first_c)

    i256, j256 = iota2(256, 256)
    spread16 = as_matrix(j256 == ((i256 // 4) % 16) * 16 + (i256 // 64) * 4 + i256 % 4)
    plane_major = as_matrix(j256 == ((i256 // 4) % 8) * 32 + (i256 // 32) * 4 + i256 % 4)
    ifold, jfold = iota2(256, 128)
    fold_lo = as_matrix(ifold % 64 == jfold)
    fold_hi = as_matrix(ifold % 64 + 64 == jfold)
    i128, j128 = iota2(128, 128)
    regroup = as_matrix(
        j128 == ((i128 // 4) % 2) * 64 + ((i128 // 8) % 2) * 32 + (i128 // 16) * 4 + i128 % 4
    )

    def unpack(half_a, half_b, whole):
        for g in range(4):
            for n, half in enumerate((half_a, half_b)):
                block = half[2 * g : 2 * g + 2].reshape(256, 256)
                rows = nn(spread16, block).astype(BF)
                for q in range(4):
                    whole[g * 64 : (g + 1) * 64, q * 512 + n * 256 : q * 512 + (n + 1) * 256] = rows[
                        q * 64 : (q + 1) * 64
                    ]

    finish(second_t, far_t)
    unpack(ta, tb, xt)
    for load in loads[:3]:
        load.wait()
    f1[:, 0:256] = nn(xt[...], gate_v[...])
    f1[:, 256:512] = nn(xt[...], up_v[...])
    low = (nt(xt[...], imaps_v[...]) * mask_v[...].astype(F32)).astype(BF)
    f1[:, 512:640] = nn(low, fold_lo)

    own = pl.ds(pl.multiple_of(c * 128, 128), 128)
    other = pl.ds(pl.multiple_of((1 - c) * 128, 128), 128)

    s1[...] = f1[other, :].astype(BF)
    core_t = send(s1, r1, tdev(1))
    far_c = third_hops(ca, second_c)
    core_t.wait_recv()
    s2[...] = (f1[own, :] + r1[...].astype(F32)).astype(BF)
    line_t = send(s2, r2, tdev(2))

    finish(second_c, far_c)
    unpack(ca, cb, ct)
    for load in loads[3:]:
        load.wait()
    f2[...] = nt(ct[...], down_v[...])
    g1[...] = f2[other, :].astype(BF)
    core_c = send(g1, gr1, tdev(1))

    line_t.wait_recv()
    total = s2[...].astype(F32) + r2[...].astype(F32)
    gate_values = total[:, 0:256]
    up_values = total[:, 256:512]
    lora_in = total[:, 512:640].astype(BF)
    wide = (nt(lora_in, fold_lo) * mask_v[own, :].astype(F32)).astype(BF)
    activated = gate_values / (1.0 + jnp.exp(-gate_values))
    act_v[...] = activated
    up_policy = up_values + nn(wide, omaps_v[...])
    e1[:, 0:256] = (activated * up_values).astype(BF)
    e1[:, 256:512] = (activated * up_policy).astype(BF)
    e1[:, 512:640] = lora_in
    pair_t = send(e1, er1, tdev(1))

    core_c.wait_recv()
    g2[...] = (f2[own, :] + gr1[...].astype(F32)).astype(BF)
    line_c = send(g2, gr2, tdev(2))

    href[own, :] = e1[:, 0:256]
    hpol[own, :] = e1[:, 256:512]
    lw_v[own, :] = wide
    pair_t.wait_recv()
    href[other, :] = er1[:, 0:256]
    hpol[other, :] = er1[:, 256:512]
    lw_v[other, :] = (nt(er1[:, 512:640], fold_lo) * mask_v[other, :].astype(F32)).astype(BF)
    hrp[...] = nn(plane_major, href[...]).astype(BF)
    hpp[...] = nn(plane_major, hpol[...]).astype(BF)

    stage1 = []
    for n, (kind, start, width) in enumerate(GROUPS):
        pair = (href, hpol) if kind == "z" else (hrp, hpp)
        for o in range(2):
            for q in range(2):
                half = width // 2
                block = nn(pair[o][...], down_v[:, start + q * half : start + (q + 1) * half]).astype(BF)
                ysend[n][:, o, :, q * half : (q + 1) * half] = block.reshape(8, 32, half)
        me = z if kind == "z" else p
        copies = []
        for k in range(1, 8):
            to = lax.rem(z + k, 8) if kind == "z" else pidx(k)
            copies.append(
                send(ysend[n].at[to], yrecv[n].at[me], zdev(k) if kind == "z" else pdev(k))
            )
        yrecv[n][me] = ysend[n][me]
        stage1.append(copies)

    line_c.wait_recv()
    grad = g2[...].astype(F32) + gr2[...].astype(F32)
    e2[...] = (grad * act_v[...]).astype(BF)
    pair_c = send(e2, er2, tdev(1))
    gup[own, :] = e2[...]
    pair_c.wait_recv()
    gup[other, :] = er2[...]

    mine = pl.ds(pl.multiple_of(t * 64, 64), 64)
    back = (nt(gup[mine, :], omaps_v[...]) * mask_v[mine, :].astype(F32)).astype(BF)
    ar0[...] = (nn(back[:32], fold_lo) + nn(back[32:], fold_hi)).astype(BF)
    ar1[p] = ar0[...]
    sum1 = [send(ar0, ar1.at[p], pdev(k)) for k in range(1, 8)]
    out_v[...] = tn(lw_v[...], gup[...])
    out_copy = pltpu.make_async_copy(out_v, out_grad, osem.at[0])
    out_copy.start()
    for copy in sum1:
        copy.wait_recv()
    ar1s[...] = jnp.sum(ar1[...].astype(F32), axis=0).astype(BF)
    ar2[z] = ar1s[...]
    sum2 = [send(ar1s, ar2.at[z], zdev(k)) for k in range(1, 8)]
    for copy in sum2:
        copy.wait_recv()
    ar2s[...] = jnp.sum(ar2[...].astype(F32), axis=0).astype(BF)
    ar3[t] = ar2s[...]
    sum3 = [send(ar2s, ar3.at[t], tdev(k)) for k in range(1, 4)]

    stage2 = []
    for n, (kind, start, width) in enumerate(GROUPS):
        half = width // 2
        for copy in stage1[n]:
            copy.wait_recv()
        pieces = []
        for q in range(2):
            for o in range(2):
                piece = yrecv[n][:, o, :, q * half : (q + 1) * half].astype(F32)
                pieces.append(jnp.sum(piece, axis=0).astype(BF))
        stacked = jnp.concatenate(pieces, axis=0)
        zsend[n][...] = nn(regroup, stacked).astype(BF).reshape(8, 16, half)
        me = p if kind == "z" else z
        copies = []
        for k in range(1, 8):
            to = pidx(k) if kind == "z" else lax.rem(z + k, 8)
            copies.append(
                send(zsend[n].at[to], zrecv[n].at[me], pdev(k) if kind == "z" else zdev(k))
            )
        zrecv[n][me] = zsend[n][me]
        stage2.append(copies)

    for copy in sum3:
        copy.wait_recv()
    wides = []
    for k in range(4):
        for fold in (fold_lo, fold_hi):
            wides.append(nt(ar3[k], fold))
    back_wide = (jnp.concatenate(wides, axis=0) * mask_v[...].astype(F32)).astype(BF)
    in_copies = []
    for k in range(4):
        in_v[:, k * 512 : (k + 1) * 512] = tn(back_wide, xt[:, k * 512 : (k + 1) * 512])
        copy = pltpu.make_async_copy(
            in_v.at[:, pl.ds(k * 512, 512)], in_grad.at[:, pl.ds(k * 512, 512)], osem.at[1 + k]
        )
        copy.start()
        in_copies.append(copy)

    i4, j16 = iota2(4, 16)
    for n, (kind, start, width) in enumerate(GROUPS):
        half = width // 2
        for copy in stage2[n]:
            copy.wait_recv()
        total = jnp.sum(zrecv[n][...].astype(F32), axis=0).astype(BF)
        for o, out in enumerate((ref_out, pol_out)):
            for q in range(2):
                pick = as_matrix(j16 == o * 8 + q * 4 + i4)
                out[:, start + q * half : start + (q + 1) * half] = nn(pick, total).astype(BF)

    out_copy.wait()
    for copy in in_copies:
        copy.wait()
    for copy in pending:
        copy.wait_send()


COPIES = 2 * (14 + 11 + 4) + 6 + 17 + 14 * len(GROUPS)


def body(tokens, token_adapter_index, gate, up, down, imaps, omaps, cotangent):
    adapters, rank, width = imaps.shape
    hidden = omaps.shape[2]
    vmem = pl.BlockSpec(memory_space=pltpu.VMEM)
    hbm = pl.BlockSpec(memory_space=pl.ANY)
    v = pltpu.VMEM
    scratch = [
        v((2048, 256), BF), v((2048, 256), BF), v((256, 2048), BF), v((256, 2048), BF), v((256, 256), BF),
        v((8, 8, 16, 256), BF), v((8, 8, 16, 256), BF), v((8, 8, 16, 256), BF), v((8, 8, 16, 256), BF),
        v((256, 2048), BF), v((256, 2048), BF),
        v((256, 640), F32), v((128, 640), BF), v((128, 640), BF), v((128, 640), BF), v((128, 640), BF),
        v((128, 640), BF), v((128, 640), BF),
        v((256, 256), F32), v((128, 256), BF), v((128, 256), BF), v((128, 256), BF), v((128, 256), BF),
        v((128, 256), BF), v((128, 256), BF),
        v((128, 256), F32), v((256, 256), BF), v((256, 256), BF), v((256, 256), BF), v((256, 256), BF),
        v((256, 256), BF), v((256, 256), BF), v((256, 256), BF),
        v((32, 128), BF), v((8, 32, 128), BF), v((32, 128), BF), v((8, 32, 128), BF), v((32, 128), BF),
        v((4, 32, 128), BF),
        v((256, 2048), F32), v((256, 256), F32),
    ]
    scratch += [v((8, 2, 32, w), BF) for _, _, w in GROUPS] * 2
    scratch += [v((8, 16, w // 2), BF) for _, _, w in GROUPS] * 2
    scratch += [
        pltpu.SemaphoreType.DMA((5,)),
        pltpu.SemaphoreType.DMA((COPIES,)),
        pltpu.SemaphoreType.DMA((COPIES,)),
        pltpu.SemaphoreType.DMA((5,)),
    ]
    ref_out, pol_out, in_grad, out_grad = pl.pallas_call(
        kernel,
        out_shape=(
            jax.ShapeDtypeStruct((4, width), BF),
            jax.ShapeDtypeStruct((4, width), BF),
            jax.ShapeDtypeStruct((adapters * rank, width), F32),
            jax.ShapeDtypeStruct((adapters * rank, hidden), F32),
        ),
        in_specs=[vmem] * 3 + [hbm] * 5,
        out_specs=(vmem, vmem, hbm, hbm),
        scratch_shapes=scratch,
        compiler_params=pltpu.CompilerParams(
            collective_id=0, has_side_effects=True, vmem_limit_bytes=56 * 2**20
        ),
        name="layer",
    )(
        token_adapter_index.reshape(1, -1),
        tokens,
        cotangent,
        gate,
        up,
        down,
        imaps.reshape(adapters * rank, width),
        omaps.reshape(adapters * rank, hidden),
    )
    return (
        ref_out,
        pol_out,
        in_grad.reshape(adapters, rank, width),
        out_grad.reshape(adapters, rank, hidden),
    )


def solution(mesh):
    in_specs = (
        P("fsdp", "tp"),
        P(),
        P("tp", "fsdp"),
        P("tp", "fsdp"),
        P("fsdp", "tp"),
        P(None, None, "tp"),
        P(None, None, "fsdp"),
        P("fsdp", "tp"),
    )
    out_specs = (P("fsdp", "tp"), P("fsdp", "tp"), P(None, None, "tp"), P(None, None, "fsdp"))
    return jax.shard_map(body, mesh=mesh, in_specs=in_specs, out_specs=out_specs, check_vma=False)
```

```python
import functools

import jax
import jax.numpy as jnp
from jax import lax
from jax.experimental import pallas as pl
from jax.experimental.pallas import tpu as pltpu
from jax.sharding import PartitionSpec as P

MESH = pl.DeviceIdType.MESH
BF = jnp.bfloat16
F32 = jnp.float32

GROUPS = (("z", 0, 768), ("p", 768, 512), ("p", 1280, 768))


def nt(a, b):
    return lax.dot_general(a, b, (((1,), (1,)), ((), ())), preferred_element_type=F32)


def tn(a, b):
    return lax.dot_general(a, b, (((0,), (0,)), ((), ())), preferred_element_type=F32)


def nn(a, b):
    return jnp.dot(a, b, preferred_element_type=F32)


def iota2(n, m):
    return (
        lax.broadcasted_iota(jnp.int32, (n, m), 0),
        lax.broadcasted_iota(jnp.int32, (n, m), 1),
    )


def as_matrix(condition):
    return condition.astype(F32).astype(BF)


def kernel(
    idx, tok, cot, gate, up, down, imaps, omaps,
    ref_out, pol_out, back_out, xt_out, wide_out, gup_out,
    gate_v, up_v, down_v, imaps_v, omaps_v,
    ta, tb, ca, cb, xt, ct,
    f1, s1, r1, s2, r2, e1, er1,
    f2, g1, gr1, g2, gr2, e2, er2,
    act_v, mask_v, lw_v, href, hpol, gup, hrp, hpp,
    ar0, ar1, ar1s, ar2, ar2s, ar3,
    *rest,
):
    ngroups = len(GROUPS)
    ysend, yrecv, zsend, zrecv = (rest[i * ngroups : (i + 1) * ngroups] for i in range(4))
    relay3, relay4, acc, wsem, ssem, rsem, osem = rest[4 * ngroups :]

    f = lax.axis_index("fsdp")
    t = lax.axis_index("tp")
    z, p, x, h, c = f // 8, f % 8, (f // 2) % 4, f % 2, t % 2

    def zdev(k):
        return {"fsdp": lax.rem(z + k + 8, 8) * 8 + p, "tp": t}

    def pidx(k):
        return lax.rem(x + k // 2, 4) * 2 + (h + k % 2) % 2

    def pdev(k):
        return {"fsdp": z * 8 + pidx(k), "tp": t}

    def tdev(k):
        return {"fsdp": f, "tp": ((t // 2 + k // 2) % 2) * 2 + (c + k % 2) % 2}

    counter = [0]
    pending = []

    def send(src, dst, device):
        n = counter[0]
        counter[0] += 1
        copy = pltpu.make_async_remote_copy(
            src_ref=src, dst_ref=dst, send_sem=ssem.at[n], recv_sem=rsem.at[n],
            device_id=device, device_id_type=MESH,
        )
        copy.start()
        pending.append(copy)
        return copy

    loads = []
    for n, (src, dst) in enumerate(
        ((gate, gate_v), (up, up_v), (imaps, imaps_v), (omaps, omaps_v), (down, down_v))
    ):
        load = pltpu.make_async_copy(src, dst, wsem.at[n])
        load.start()
        loads.append(load)

    barrier = pltpu.get_barrier_semaphore()
    partners = [zdev(k) for k in range(1, 8)] + [pdev(k) for k in range(1, 8)] + [tdev(k) for k in range(1, 4)]
    for device in partners:
        pl.semaphore_signal(barrier, 1, device_id=device, device_id_type=MESH)

    i16, j4 = iota2(16, 4)
    for src, half_a, half_b in ((tok, ta, tb), (cot, ca, cb)):
        packed = None
        for q in range(4):
            spread = as_matrix(i16 == q * 4 + j4)
            term = nn(spread, src[:, q * 512 : (q + 1) * 512])
            packed = term if packed is None else packed + term
        packed = packed.astype(BF)
        half_a[z, p] = packed[:, :256]
        half_b[z, p] = packed[:, 256:]

    i8, j8 = iota2(8, 256)
    chosen = as_matrix(idx[...] == i8)
    mask_v[...] = tn(chosen, as_matrix(i8 == j8 // 64)).astype(BF)

    pl.semaphore_wait(barrier, len(partners))

    def first_hops(half_a, half_b):
        a = [send(half_a.at[z, p], half_a.at[z, p], pdev(k)) for k in range(1, 8)]
        b = [send(half_b.at[z, p], half_b.at[z, p], zdev(k)) for k in range(1, 8)]
        return a, b

    def second_hops(half_a, half_b, first):
        a, b = first
        for copy in a:
            copy.wait_recv()
        near = [send(half_a.at[z], half_a.at[z], zdev(k)) for k in (2, -2, 1, -1)]
        for copy in b:
            copy.wait_recv()
        plane = [send(half_b.at[:, p], half_b.at[:, p], pdev(k)) for k in range(1, 8)]
        return near, plane

    def third_hops(half_a, second):
        near, _ = second
        far = []
        for n, sign in ((0, 1), (1, -1)):
            near[n].wait_recv()
            block = lax.rem(z - 2 * sign + 8, 8)
            part = half_a.at[block, pl.ds(0 if sign == 1 else 4, 4)]
            far.append(send(part, part, zdev(2 * sign)))
            far.append(send(half_a.at[block], half_a.at[block], zdev(sign)))
        return far

    def finish(second, far):
        near, plane = second
        for copy in near[2:] + plane + far:
            copy.wait_recv()

    first_t = first_hops(ta, tb)
    first_c = first_hops(ca, cb)
    second_t = second_hops(ta, tb, first_t)
    far_t = third_hops(ta, second_t)
    second_c = second_hops(ca, cb, first_c)

    i256, j256 = iota2(256, 256)
    spread16 = as_matrix(j256 == ((i256 // 4) % 16) * 16 + (i256 // 64) * 4 + i256 % 4)
    plane_major = as_matrix(j256 == ((i256 // 4) % 8) * 32 + (i256 // 32) * 4 + i256 % 4)
    ifold, jfold = iota2(256, 128)
    fold_lo = as_matrix(ifold % 64 == jfold)
    fold_hi = as_matrix(ifold % 64 + 64 == jfold)
    i128, j128 = iota2(128, 128)
    regroup = as_matrix(
        j128 == ((i128 // 4) % 2) * 64 + ((i128 // 8) % 2) * 32 + (i128 // 16) * 4 + i128 % 4
    )

    def unpack(half_a, half_b, whole):
        for g in range(4):
            for n, half in enumerate((half_a, half_b)):
                block = half[2 * g : 2 * g + 2].reshape(256, 256)
                rows = nn(spread16, block).astype(BF)
                for q in range(4):
                    whole[g * 64 : (g + 1) * 64, q * 512 + n * 256 : q * 512 + (n + 1) * 256] = rows[
                        q * 64 : (q + 1) * 64
                    ]

    finish(second_t, far_t)
    unpack(ta, tb, xt)
    xt_copy = pltpu.make_async_copy(xt, xt_out, osem.at[0])
    xt_copy.start()
    for load in loads[:3]:
        load.wait()
    f1[:, 0:256] = nn(xt[...], gate_v[...])
    f1[:, 256:512] = nn(xt[...], up_v[...])
    low = (nt(xt[...], imaps_v[...]) * mask_v[...].astype(F32)).astype(BF)
    f1[:, 512:640] = nn(low, fold_lo)

    own = pl.ds(pl.multiple_of(c * 128, 128), 128)
    other = pl.ds(pl.multiple_of((1 - c) * 128, 128), 128)

    s1[...] = f1[other, :].astype(BF)
    core_t = send(s1, r1, tdev(1))
    far_c = third_hops(ca, second_c)

    core_t.wait_recv()
    s2[...] = (f1[own, :] + r1[...].astype(F32)).astype(BF)
    line_t = send(s2, r2, tdev(2))
    finish(second_c, far_c)
    unpack(ca, cb, ct)
    for load in loads[3:]:
        load.wait()
    f2[...] = nt(ct[...], down_v[...])
    g1[...] = f2[other, :].astype(BF)
    core_c = send(g1, gr1, tdev(1))

    line_t.wait_recv()
    total = s2[...].astype(F32) + r2[...].astype(F32)
    gate_values = total[:, 0:256]
    up_values = total[:, 256:512]
    lora_in = total[:, 512:640].astype(BF)
    wide = (nt(lora_in, fold_lo) * mask_v[own, :].astype(F32)).astype(BF)
    activated = gate_values / (1.0 + jnp.exp(-gate_values))
    act_v[...] = activated
    up_policy = up_values + nn(wide, omaps_v[...])
    e1[:, 0:256] = (activated * up_values).astype(BF)
    e1[:, 256:512] = (activated * up_policy).astype(BF)
    e1[:, 512:640] = lora_in
    pair_t = send(e1, er1, tdev(1))

    core_c.wait_recv()
    g2[...] = (f2[own, :] + gr1[...].astype(F32)).astype(BF)
    line_c = send(g2, gr2, tdev(2))

    href[own, :] = e1[:, 0:256]
    hpol[own, :] = e1[:, 256:512]
    lw_v[own, :] = wide
    pair_t.wait_recv()
    href[other, :] = er1[:, 0:256]
    hpol[other, :] = er1[:, 256:512]
    lw_v[other, :] = (nt(er1[:, 512:640], fold_lo) * mask_v[other, :].astype(F32)).astype(BF)
    hrp[...] = nn(plane_major, href[...]).astype(BF)
    hpp[...] = nn(plane_major, hpol[...]).astype(BF)

    stage1 = []

    def first_stage(n):
        kind, start, width = GROUPS[n]
        pair = (href, hpol) if kind == "z" else (hrp, hpp)
        half = width // 2
        for o in range(2):
            for q in range(2):
                block = nn(pair[o][...], down_v[:, start + q * half : start + (q + 1) * half]).astype(BF)
                ysend[n][:, o, :, q * half : (q + 1) * half] = block.reshape(8, 32, half)
        copies = []
        if kind == "z":
            for m, sign in ((0, 1), (1, -1)):
                copies.append(send(ysend[n].at[lax.rem(z + 3 * sign + 8, 8)], relay3.at[m], zdev(sign)))
                copies.append(send(ysend[n].at[lax.rem(z + 4, 8), m], relay4.at[m], zdev(2 * sign)))
            for m, sign in ((0, 1), (1, -1)):
                copies.append(send(ysend[n].at[lax.rem(z + sign + 8, 8)], yrecv[n].at[m], zdev(sign)))
        else:
            for k in range(1, 8):
                copies.append(send(ysend[n].at[pidx(k)], yrecv[n].at[p], pdev(k)))
            yrecv[n][p] = ysend[n][p]
        stage1.append(copies)

    first_stage(0)
    first_stage(1)

    line_c.wait_recv()
    grad = g2[...].astype(F32) + gr2[...].astype(F32)
    e2[...] = (grad * act_v[...]).astype(BF)
    pair_c = send(e2, er2, tdev(1))
    gup[own, :] = e2[...]
    pair_c.wait_recv()
    gup[other, :] = er2[...]

    wide_copy = pltpu.make_async_copy(lw_v, wide_out, osem.at[1])
    wide_copy.start()
    gup_copy = pltpu.make_async_copy(gup, gup_out, osem.at[2])
    gup_copy.start()
    mine = pl.ds(pl.multiple_of(t * 64, 64), 64)
    back = (nt(gup[mine, :], omaps_v[...]) * mask_v[mine, :].astype(F32)).astype(BF)
    ar0[...] = (nn(back[:32], fold_lo) + nn(back[32:], fold_hi)).astype(BF)
    ar1[p] = ar0[...]
    sum1 = [send(ar0, ar1.at[p], pdev(k)) for k in range(1, 8)]

    first_stage(2)
    for n in range(4):
        stage1[0][n].wait_recv()
    for m, sign in ((0, 1), (1, -1)):
        block = ysend[0][lax.rem(z + 2 * sign + 8, 8)].astype(F32) + relay3[m].astype(F32)
        acc[m, m] = (block[m] + relay4[m].astype(F32)).astype(BF)
        acc[m, 1 - m] = block[1 - m].astype(BF)
        stage1[0].append(send(acc.at[m], yrecv[0].at[2 + m], zdev(2 * sign)))

    stage2 = []

    def second_stage(n):
        kind, start, width = GROUPS[n]
        half = width // 2
        for copy in stage1[n][4:] if kind == "z" else stage1[n]:
            copy.wait_recv()
        pieces = []
        for q in range(2):
            for o in range(2):
                columns = slice(q * half, (q + 1) * half)
                piece = jnp.sum(yrecv[n][:, o, :, columns].astype(F32), axis=0)
                if kind == "z":
                    piece = piece + ysend[n][z, o, :, columns].astype(F32)
                pieces.append(piece.astype(BF))
        stacked = jnp.concatenate(pieces, axis=0)
        zsend[n][...] = nn(regroup, stacked).astype(BF).reshape(8, 16, half)
        me = p if kind == "z" else z
        copies = []
        for k in range(1, 8):
            to = pidx(k) if kind == "z" else lax.rem(z + k, 8)
            copies.append(
                send(zsend[n].at[to], zrecv[n].at[me], pdev(k) if kind == "z" else zdev(k))
            )
        zrecv[n][me] = zsend[n][me]
        stage2.append(copies)

    for copy in sum1:
        copy.wait_recv()
    ar1s[...] = jnp.sum(ar1[...].astype(F32), axis=0).astype(BF)
    ar2[z] = ar1s[...]
    sum2 = [send(ar1s, ar2.at[z], zdev(k)) for k in range(1, 8)]
    second_stage(0)
    second_stage(1)
    for copy in sum2:
        copy.wait_recv()
    ar2s[...] = jnp.sum(ar2[...].astype(F32), axis=0).astype(BF)
    ar3[t] = ar2s[...]
    sum3 = [send(ar2s, ar3.at[t], tdev(k)) for k in range(1, 4)]
    second_stage(2)
    for copy in sum3:
        copy.wait_recv()
    wides = []
    for k in range(4):
        for fold in (fold_lo, fold_hi):
            wides.append(nt(ar3[k], fold))
    back_out[...] = (jnp.concatenate(wides, axis=0) * mask_v[...].astype(F32)).astype(BF)

    i4, j16 = iota2(4, 16)
    for n, (kind, start, width) in enumerate(GROUPS):
        half = width // 2
        for copy in stage2[n]:
            copy.wait_recv()
        total = jnp.sum(zrecv[n][...].astype(F32), axis=0).astype(BF)
        for o, out in enumerate((ref_out, pol_out)):
            for q in range(2):
                pick = as_matrix(j16 == o * 8 + q * 4 + i4)
                out[:, start + q * half : start + (q + 1) * half] = nn(pick, total).astype(BF)

    for copy in (xt_copy, wide_copy, gup_copy):
        copy.wait()
    for copy in pending:
        copy.wait_send()


def gradients(
    ref_in, pol_in, back, wide, gup, xt, ref_out, pol_out, in_grad, out_grad,
    rv, pv, bv, wv, uv, xv, gv, ov, isem, osem,
):
    sources = [back, wide, gup, ref_in, pol_in] + [xt.at[:, pl.ds(k * 512, 512)] for k in range(4)]
    places = [bv, wv, uv, rv, pv] + [xv.at[k] for k in range(4)]
    loads = []
    for n in range(9):
        load = pltpu.make_async_copy(sources[n], places[n], isem.at[n])
        load.start()
        loads.append(load)
    stores = []

    def store(src, dst):
        copy = pltpu.make_async_copy(src, dst, osem.at[len(stores)])
        copy.start()
        stores.append(copy)

    loads[0].wait()
    for k in range(4):
        loads[5 + k].wait()
        gv[k] = tn(bv[...], xv[k])
        store(gv.at[k], in_grad.at[:, pl.ds(k * 512, 512)])
    for n in (1, 2, 3, 4):
        loads[n].wait()
    store(rv, ref_out)
    store(pv, pol_out)
    ov[...] = tn(wv[...], uv[...])
    store(ov, out_grad)
    for copy in stores:
        copy.wait()


COPIES = 2 * (14 + 11 + 4) + 6 + 17 + 14 * len(GROUPS) + 1


def body(tokens, token_adapter_index, gate, up, down, imaps, omaps, cotangent):
    adapters, rank, width = imaps.shape
    hidden = omaps.shape[2]
    vmem = pl.BlockSpec(memory_space=pltpu.VMEM)
    hbm = pl.BlockSpec(memory_space=pl.ANY)
    v = pltpu.VMEM
    scratch = [
        v((2048, 256), BF), v((2048, 256), BF), v((256, 2048), BF), v((256, 2048), BF), v((256, 256), BF),
        v((8, 8, 16, 256), BF), v((8, 8, 16, 256), BF), v((8, 8, 16, 256), BF), v((8, 8, 16, 256), BF),
        v((256, 2048), BF), v((256, 2048), BF),
        v((256, 640), F32), v((128, 640), BF), v((128, 640), BF), v((128, 640), BF), v((128, 640), BF),
        v((128, 640), BF), v((128, 640), BF),
        v((256, 256), F32), v((128, 256), BF), v((128, 256), BF), v((128, 256), BF), v((128, 256), BF),
        v((128, 256), BF), v((128, 256), BF),
        v((128, 256), F32), v((256, 256), BF), v((256, 256), BF), v((256, 256), BF), v((256, 256), BF),
        v((256, 256), BF), v((256, 256), BF), v((256, 256), BF),
        v((32, 128), BF), v((8, 32, 128), BF), v((32, 128), BF), v((8, 32, 128), BF), v((32, 128), BF),
        v((4, 32, 128), BF),
    ]
    scratch += [v((8, 2, 32, w), BF) for _, _, w in GROUPS]
    scratch += [v((4 if kind == "z" else 8, 2, 32, w), BF) for kind, _, w in GROUPS]
    scratch += [v((8, 16, w // 2), BF) for _, _, w in GROUPS] * 2
    first = GROUPS[0][2]
    scratch += [v((2, 2, 32, first), BF), v((2, 32, first), BF), v((2, 2, 32, first), BF)]
    scratch += [
        pltpu.SemaphoreType.DMA((5,)),
        pltpu.SemaphoreType.DMA((COPIES,)),
        pltpu.SemaphoreType.DMA((COPIES,)),
        pltpu.SemaphoreType.DMA((3,)),
    ]
    ref_out, pol_out, back, xt, wide, gup = pl.pallas_call(
        kernel,
        out_shape=(
            jax.ShapeDtypeStruct((4, width), BF),
            jax.ShapeDtypeStruct((4, width), BF),
            jax.ShapeDtypeStruct((256, 256), BF),
            jax.ShapeDtypeStruct((256, width), BF),
            jax.ShapeDtypeStruct((256, 256), BF),
            jax.ShapeDtypeStruct((256, 256), BF),
        ),
        in_specs=[vmem] * 3 + [hbm] * 5,
        out_specs=(vmem, vmem, vmem, hbm, hbm, hbm),
        scratch_shapes=scratch,
        compiler_params=pltpu.CompilerParams(
            collective_id=0, has_side_effects=True, vmem_limit_bytes=56 * 2**20
        ),
        name="layer",
    )(
        token_adapter_index.reshape(1, -1),
        tokens,
        cotangent,
        gate,
        up,
        down,
        imaps.reshape(adapters * rank, width),
        omaps.reshape(adapters * rank, hidden),
    )
    ref_out, pol_out, in_grad, out_grad = pl.pallas_call(
        gradients,
        out_shape=(
            jax.ShapeDtypeStruct((4, width), BF),
            jax.ShapeDtypeStruct((4, width), BF),
            jax.ShapeDtypeStruct((adapters * rank, width), F32),
            jax.ShapeDtypeStruct((adapters * rank, hidden), F32),
        ),
        in_specs=[hbm] * 6,
        out_specs=(hbm,) * 4,
        scratch_shapes=[
            v((4, width), BF), v((4, width), BF), v((256, 256), BF), v((256, 256), BF), v((256, 256), BF),
            v((4, 256, 512), BF), v((4, 256, 512), F32), v((256, 256), F32),
            pltpu.SemaphoreType.DMA((9,)), pltpu.SemaphoreType.DMA((7,)),
        ],
        compiler_params=pltpu.CompilerParams(vmem_limit_bytes=60 * 2**20),
        name="gradients",
    )(ref_out, pol_out, back, wide, gup, xt)
    return (
        ref_out,
        pol_out,
        in_grad.reshape(adapters, rank, width),
        out_grad.reshape(adapters, rank, hidden),
    )


def solution(mesh):
    in_specs = (
        P("fsdp", "tp"),
        P(),
        P("tp", "fsdp"),
        P("tp", "fsdp"),
        P("fsdp", "tp"),
        P(None, None, "tp"),
        P(None, None, "fsdp"),
        P("fsdp", "tp"),
    )
    out_specs = (P("fsdp", "tp"), P("fsdp", "tp"), P(None, None, "tp"), P(None, None, "fsdp"))
    return jax.shard_map(body, mesh=mesh, in_specs=in_specs, out_specs=out_specs, check_vma=False)
```

```python
import functools

import jax
import jax.numpy as jnp
from jax import lax
from jax.experimental import pallas as pl
from jax.experimental.pallas import tpu as pltpu
from jax.sharding import PartitionSpec as P

MESH = pl.DeviceIdType.MESH
BF = jnp.bfloat16
F32 = jnp.float32

GROUPS = (("z", 0, 1024), ("p", 1024, 512), ("p", 1536, 512))


Z_STEPS = (4, 3, 5, 2, 6, 1, 7)
P_STEPS = (5, 3, 7, 1, 4, 2, 6)


def nt(a, b):
    return lax.dot_general(a, b, (((1,), (1,)), ((), ())), preferred_element_type=F32)


def tn(a, b):
    return lax.dot_general(a, b, (((0,), (0,)), ((), ())), preferred_element_type=F32)


def nn(a, b):
    return jnp.dot(a, b, preferred_element_type=F32)


def iota2(n, m):
    return (
        lax.broadcasted_iota(jnp.int32, (n, m), 0),
        lax.broadcasted_iota(jnp.int32, (n, m), 1),
    )


def as_matrix(condition):
    return condition.astype(F32).astype(BF)


def kernel(
    idx, tok, cot, gate, up, down, imaps, omaps,
    ref_out, pol_out, back_out, xt_out, wide_out, gup_out,
    gate_v, up_v, down_v, imaps_v, omaps_v,
    ta, tb, ca, cb, xt, ct,
    f1, s1, r1, s2, r2, e1, er1,
    f2, g1, gr1, g2, gr2, e2, er2,
    act_v, mask_v, lw_v, href, hpol, gup, hrp, hpp,
    ar0, ar1, ar1s, ar2, ar2s, ar3,
    *rest,
):
    ngroups = len(GROUPS)
    ysend, yrecv, zsend, zrecv = (rest[i * ngroups : (i + 1) * ngroups] for i in range(4))
    relay3, relay4, acc, wsem, ssem, rsem, osem = rest[4 * ngroups :]

    f = lax.axis_index("fsdp")
    t = lax.axis_index("tp")
    z, p, x, h, c = f // 8, f % 8, (f // 2) % 4, f % 2, t % 2

    def zdev(k):
        return {"fsdp": lax.rem(z + k + 8, 8) * 8 + p, "tp": t}

    def pidx(k):
        return lax.rem(x + k // 2, 4) * 2 + (h + k % 2) % 2

    def pdev(k):
        return {"fsdp": z * 8 + pidx(k), "tp": t}

    def tdev(k):
        return {"fsdp": f, "tp": ((t // 2 + k // 2) % 2) * 2 + (c + k % 2) % 2}

    counter = [0]
    pending = []

    def send(src, dst, device):
        n = counter[0]
        counter[0] += 1
        copy = pltpu.make_async_remote_copy(
            src_ref=src, dst_ref=dst, send_sem=ssem.at[n], recv_sem=rsem.at[n],
            device_id=device, device_id_type=MESH,
        )
        copy.start()
        pending.append(copy)
        return copy

    loads = []
    for n, (src, dst) in enumerate(
        ((gate, gate_v), (up, up_v), (imaps, imaps_v), (omaps, omaps_v), (down, down_v))
    ):
        load = pltpu.make_async_copy(src, dst, wsem.at[n])
        load.start()
        loads.append(load)

    barrier = pltpu.get_barrier_semaphore()
    partners = [zdev(k) for k in Z_STEPS] + [pdev(k) for k in P_STEPS] + [tdev(k) for k in range(1, 4)]
    for device in partners:
        pl.semaphore_signal(barrier, 1, device_id=device, device_id_type=MESH)

    i16, j4 = iota2(16, 4)
    for src, half_a, half_b in ((tok, ta, tb), (cot, ca, cb)):
        packed = None
        for q in range(4):
            spread = as_matrix(i16 == q * 4 + j4)
            term = nn(spread, src[:, q * 512 : (q + 1) * 512])
            packed = term if packed is None else packed + term
        packed = packed.astype(BF)
        half_a[z, p] = packed[:, :256]
        half_b[z, p] = packed[:, 256:]

    i8, j8 = iota2(8, 256)
    i256, j256 = iota2(256, 256)
    chosen = as_matrix(idx[...] == i8)
    order = as_matrix(j256 == ((i256 // 2) % 64) * 4 + (i256 // 128) * 2 + i256 % 2)
    mask_v[...] = nn(order, tn(chosen, as_matrix(i8 == j8 // 64)).astype(BF)).astype(BF)

    pl.semaphore_wait(barrier, len(partners))

    def first_hops(half_a, half_b):
        a = [send(half_a.at[z, p], half_a.at[z, p], pdev(k)) for k in P_STEPS]
        b = [send(half_b.at[z, p], half_b.at[z, p], zdev(k)) for k in Z_STEPS]
        return a, b

    def near_hops(half_a):
        return [send(half_a.at[z], half_a.at[z], zdev(k)) for k in (2, -2, 1, -1)]

    def plane_hops(half_b):
        return [send(half_b.at[:, p], half_b.at[:, p], pdev(k)) for k in P_STEPS]

    def far_hops(half_a, near):
        far = []
        for n, sign in ((0, 1), (1, -1)):
            near[n].wait_recv()
            block = lax.rem(z - 2 * sign + 8, 8)
            part = half_a.at[block, pl.ds(0 if sign == 1 else 4, 4)]
            far.append(send(part, part, zdev(2 * sign)))
            far.append(send(half_a.at[block], half_a.at[block], zdev(sign)))
        return far

    def arrived(copies):
        for copy in copies:
            copy.wait_recv()

    first_t = first_hops(ta, tb)
    first_c = first_hops(ca, cb)
    arrived(first_t[0])
    near_t = near_hops(ta)
    arrived(first_t[1])
    plane_t = plane_hops(tb)

    spread16 = as_matrix(
        j256 == ((i256 // 2) % 16) * 16 + (i256 // 64) * 4 + ((i256 // 32) % 2) * 2 + i256 % 2
    )
    i128, j128 = iota2(128, 128)
    plane_major = as_matrix(j128 == ((i128 // 2) % 8) * 16 + (i128 // 16) * 2 + i128 % 2)
    ifold, jfold = iota2(256, 128)
    fold_lo = as_matrix(ifold % 64 == jfold)
    fold_hi = as_matrix(ifold % 64 + 64 == jfold)
    regroup = as_matrix(
        j128
        == ((i128 // 4) % 2) * 64 + ((i128 // 8) % 2) * 32 + ((i128 // 2) % 2) * 16 + (i128 // 16) * 2 + i128 % 2
    )

    far_t = far_hops(ta, near_t)
    arrived(first_c[0])
    near_c = near_hops(ca)
    arrived(first_c[1])
    plane_c = plane_hops(cb)

    def unpack(half, n, whole):
        for g in range(4):
            block = nn(spread16, half[2 * g : 2 * g + 2].reshape(256, 256)).astype(BF)
            for q in range(4):
                for j in range(2):
                    whole[j * 128 + g * 32 : j * 128 + (g + 1) * 32, q * 512 + n * 256 : q * 512 + (n + 1) * 256] = (
                        block[q * 64 + j * 32 : q * 64 + (j + 1) * 32]
                    )

    rows = [slice(j * 128, (j + 1) * 128) for j in range(2)]
    own = [pl.ds(pl.multiple_of(j * 128 + c * 64, 64), 64) for j in range(2)]
    other = [pl.ds(pl.multiple_of(j * 128 + (1 - c) * 64, 64), 64) for j in range(2)]

    def to_line(j, copy):
        copy.wait_recv()
        s2[j] = (f1[own[j], :] + r1[j].astype(F32)).astype(BF)
        return send(s2.at[j], r2.at[j], tdev(2))

    arrived(plane_t)
    unpack(tb, 1, xt)
    for load in loads[:3]:
        load.wait()
    arrived(near_t[2:] + far_t)
    unpack(ta, 0, xt)
    f1[:, 0:256] = nn(xt[...], gate_v[...])
    f1[:, 256:512] = nn(xt[...], up_v[...])
    low = (nt(xt[...], imaps_v[...]) * mask_v[...].astype(F32)).astype(BF)
    f1[:, 512:640] = nn(low, fold_lo)
    core_t = []
    for j in range(2):
        s1[j] = f1[other[j], :].astype(BF)
        core_t.append(send(s1.at[j], r1.at[j], tdev(1)))
    xt_copy = pltpu.make_async_copy(xt, xt_out, osem.at[0])
    xt_copy.start()
    line_0 = to_line(0, core_t[0])
    line_1 = to_line(1, core_t[1])
    far_c = far_hops(ca, near_c)

    for load in loads[3:]:
        load.wait()

    def activate(j, copy):
        copy.wait_recv()
        total = s2[j].astype(F32) + r2[j].astype(F32)
        gate_values = total[:, 0:256]
        up_values = total[:, 256:512]
        lora_in = total[:, 512:640].astype(BF)
        wide = (nt(lora_in, fold_lo) * mask_v[own[j], :].astype(F32)).astype(BF)
        activated = gate_values / (1.0 + jnp.exp(-gate_values))
        act_v[j] = activated
        up_policy = up_values + nn(wide, omaps_v[...])
        e1[j, :, 0:256] = (activated * up_values).astype(BF)
        e1[j, :, 256:512] = (activated * up_policy).astype(BF)
        e1[j, :, 512:640] = lora_in
        pair = send(e1.at[j], er1.at[j], tdev(1))
        href[own[j], :] = e1[j, :, 0:256]
        hpol[own[j], :] = e1[j, :, 256:512]
        lw_v[own[j], :] = wide
        return pair

    def collect(j, copy):
        copy.wait_recv()
        href[other[j], :] = er1[j, :, 0:256]
        hpol[other[j], :] = er1[j, :, 256:512]
        lw_v[other[j], :] = (nt(er1[j, :, 512:640], fold_lo) * mask_v[other[j], :].astype(F32)).astype(BF)
        hrp[rows[j], :] = nn(plane_major, href[rows[j], :]).astype(BF)
        hpp[rows[j], :] = nn(plane_major, hpol[rows[j], :]).astype(BF)

    stage1 = [[[], []] for _ in GROUPS]

    def first_stage(n, j):
        kind, start, width = GROUPS[n]
        pair = (href, hpol) if kind == "z" else (hrp, hpp)
        half = width // 2
        for o in range(2):
            for q in range(2):
                block = nn(pair[o][rows[j], :], down_v[:, start + q * half : start + (q + 1) * half]).astype(BF)
                ysend[n][j, :, o, :, q * half : (q + 1) * half] = block.reshape(8, 16, half)
        copies = stage1[n][j]
        if kind == "z":
            for m, sign in ((0, 1), (1, -1)):
                copies.append(send(ysend[n].at[j, lax.rem(z + 3 * sign + 8, 8)], relay3.at[j, m], zdev(sign)))
                copies.append(send(ysend[n].at[j, lax.rem(z + 4, 8), m], relay4.at[j, m], zdev(2 * sign)))
            for m, sign in ((0, 1), (1, -1)):
                copies.append(send(ysend[n].at[j, lax.rem(z + sign + 8, 8)], yrecv[n].at[j, m], zdev(sign)))
        else:
            for k in P_STEPS:
                copies.append(send(ysend[n].at[j, pidx(k)], yrecv[n].at[j, p], pdev(k)))
            yrecv[n][j, p] = ysend[n][j, p]

    def relay(j):
        arrived(stage1[0][j][:4])
        for m, sign in ((0, 1), (1, -1)):
            block = ysend[0][j, lax.rem(z + 2 * sign + 8, 8)].astype(F32) + relay3[j, m].astype(F32)
            acc[j, m, m] = (block[m] + relay4[j, m].astype(F32)).astype(BF)
            acc[j, m, 1 - m] = block[1 - m].astype(BF)
            stage1[0][j].append(send(acc.at[j, m], yrecv[0].at[j, 2 + m], zdev(2 * sign)))

    pair_0 = activate(0, line_0)
    pair_1 = activate(1, line_1)
    arrived(near_c[2:] + plane_c + far_c)
    unpack(ca, 0, ct)
    unpack(cb, 1, ct)
    f2[...] = nt(ct[...], down_v[...])
    for j in range(2):
        g1[j] = f2[other[j], :].astype(BF)
    core_c = send(g1, gr1, tdev(1))
    collect(0, pair_0)
    first_stage(0, 0)
    core_c.wait_recv()
    for j in range(2):
        g2[j] = (f2[own[j], :] + gr1[j].astype(F32)).astype(BF)
    line_c = send(g2, gr2, tdev(2))
    first_stage(1, 0)
    collect(1, pair_1)
    first_stage(0, 1)
    relay(0)
    first_stage(1, 1)
    line_c.wait_recv()
    e2[...] = ((g2[...].astype(F32) + gr2[...].astype(F32)) * act_v[...]).astype(BF)
    mine = pl.ds(pl.multiple_of(t * 64, 64), 64)
    back = (nt(e2[t // 2], omaps_v[...]) * mask_v[mine, :].astype(F32)).astype(BF)
    ar0[...] = (nn(back[:32], fold_lo) + nn(back[32:], fold_hi)).astype(BF)
    sum1 = [send(ar0, ar1.at[p], pdev(k)) for k in P_STEPS]
    pair_c = send(e2, er2, tdev(1))
    ar1[p] = ar0[...]
    first_stage(2, 0)
    first_stage(2, 1)
    relay(1)

    stage2 = []

    def second_stage(n):
        kind, start, width = GROUPS[n]
        half = width // 2
        for j in range(2):
            arrived(stage1[n][j][4:] if kind == "z" else stage1[n][j])
        pieces = []
        for q in range(2):
            for o in range(2):
                columns = slice(q * half, (q + 1) * half)
                for j in range(2):
                    piece = jnp.sum(yrecv[n][j, :, o, :, columns].astype(F32), axis=0)
                    if kind == "z":
                        piece = piece + ysend[n][j, z, o, :, columns].astype(F32)
                    pieces.append(piece.astype(BF))
        stacked = jnp.concatenate(pieces, axis=0)
        zsend[n][...] = nn(regroup, stacked).astype(BF).reshape(8, 16, half)
        me = p if kind == "z" else z
        copies = []
        for k in P_STEPS if kind == "z" else Z_STEPS:
            to = pidx(k) if kind == "z" else lax.rem(z + k, 8)
            copies.append(
                send(zsend[n].at[to], zrecv[n].at[me], pdev(k) if kind == "z" else zdev(k))
            )
        zrecv[n][me] = zsend[n][me]
        stage2.append(copies)

    for copy in sum1:
        copy.wait_recv()
    ar1s[...] = jnp.sum(ar1[...].astype(F32), axis=0).astype(BF)
    ar2[z] = ar1s[...]
    sum2 = [send(ar1s, ar2.at[z], zdev(k)) for k in Z_STEPS]
    for j in range(2):
        gup[own[j], :] = e2[j]
    pair_c.wait_recv()
    for j in range(2):
        gup[other[j], :] = er2[j]
    wide_copy = pltpu.make_async_copy(lw_v, wide_out, osem.at[1])
    wide_copy.start()
    gup_copy = pltpu.make_async_copy(gup, gup_out, osem.at[2])
    gup_copy.start()
    second_stage(0)
    second_stage(1)
    for copy in sum2:
        copy.wait_recv()
    ar2s[...] = jnp.sum(ar2[...].astype(F32), axis=0).astype(BF)
    ar3[t] = ar2s[...]
    sum3 = [send(ar2s, ar3.at[t], tdev(k)) for k in range(1, 4)]
    second_stage(2)
    for copy in sum3:
        copy.wait_recv()
    wides = []
    for k in range(4):
        for fold in (fold_lo, fold_hi):
            wides.append(nt(ar3[k], fold))
    back_out[...] = (jnp.concatenate(wides, axis=0) * mask_v[...].astype(F32)).astype(BF)

    i4, j16 = iota2(4, 16)
    for n, (kind, start, width) in enumerate(GROUPS):
        half = width // 2
        for copy in stage2[n]:
            copy.wait_recv()
        total = jnp.sum(zrecv[n][...].astype(F32), axis=0).astype(BF)
        for o, out in enumerate((ref_out, pol_out)):
            for q in range(2):
                pick = as_matrix(j16 == o * 8 + q * 4 + i4)
                out[:, start + q * half : start + (q + 1) * half] = nn(pick, total).astype(BF)

    for copy in (xt_copy, wide_copy, gup_copy):
        copy.wait()
    for copy in pending:
        copy.wait_send()


def gradients(
    ref_in, pol_in, back, wide, gup, xt, ref_out, pol_out, in_grad, out_grad,
    rv, pv, bv, wv, uv, xv, gv, ov, isem, osem,
):
    sources = [back, wide, gup, ref_in, pol_in] + [xt.at[:, pl.ds(k * 512, 512)] for k in range(4)]
    places = [bv, wv, uv, rv, pv] + [xv.at[k] for k in range(4)]
    loads = []
    for n in range(9):
        load = pltpu.make_async_copy(sources[n], places[n], isem.at[n])
        load.start()
        loads.append(load)
    stores = []

    def store(src, dst):
        copy = pltpu.make_async_copy(src, dst, osem.at[len(stores)])
        copy.start()
        stores.append(copy)

    loads[0].wait()
    for k in range(4):
        loads[5 + k].wait()
        gv[k] = tn(bv[...], xv[k])
        store(gv.at[k], in_grad.at[:, pl.ds(k * 512, 512)])
    for n in (1, 2, 3, 4):
        loads[n].wait()
    store(rv, ref_out)
    store(pv, pol_out)
    ov[...] = tn(wv[...], uv[...])
    store(ov, out_grad)
    for copy in stores:
        copy.wait()


COPIES = 2 * (14 + 11 + 4) + 6 + 3 + 16 + 28 + 21 + 17


def body(tokens, token_adapter_index, gate, up, down, imaps, omaps, cotangent):
    adapters, rank, width = imaps.shape
    hidden = omaps.shape[2]
    vmem = pl.BlockSpec(memory_space=pltpu.VMEM)
    hbm = pl.BlockSpec(memory_space=pl.ANY)
    v = pltpu.VMEM
    scratch = [
        v((2048, 256), BF), v((2048, 256), BF), v((256, 2048), BF), v((256, 2048), BF), v((256, 256), BF),
        v((8, 8, 16, 256), BF), v((8, 8, 16, 256), BF), v((8, 8, 16, 256), BF), v((8, 8, 16, 256), BF),
        v((256, 2048), BF), v((256, 2048), BF),
        v((256, 640), F32), v((2, 64, 640), BF), v((2, 64, 640), BF), v((2, 64, 640), BF), v((2, 64, 640), BF),
        v((2, 64, 640), BF), v((2, 64, 640), BF),
        v((256, 256), F32), v((2, 64, 256), BF), v((2, 64, 256), BF), v((2, 64, 256), BF), v((2, 64, 256), BF),
        v((2, 64, 256), BF), v((2, 64, 256), BF),
        v((2, 64, 256), F32), v((256, 256), BF), v((256, 256), BF), v((256, 256), BF), v((256, 256), BF),
        v((256, 256), BF), v((256, 256), BF), v((256, 256), BF),
        v((32, 128), BF), v((8, 32, 128), BF), v((32, 128), BF), v((8, 32, 128), BF), v((32, 128), BF),
        v((4, 32, 128), BF),
    ]
    scratch += [v((2, 8, 2, 16, w), BF) for _, _, w in GROUPS]
    scratch += [v((2, 4 if kind == "z" else 8, 2, 16, w), BF) for kind, _, w in GROUPS]
    scratch += [v((8, 16, w // 2), BF) for _, _, w in GROUPS] * 2
    first = GROUPS[0][2]
    scratch += [v((2, 2, 2, 16, first), BF), v((2, 2, 16, first), BF), v((2, 2, 2, 16, first), BF)]
    scratch += [
        pltpu.SemaphoreType.DMA((5,)),
        pltpu.SemaphoreType.DMA((COPIES,)),
        pltpu.SemaphoreType.DMA((COPIES,)),
        pltpu.SemaphoreType.DMA((3,)),
    ]
    ref_out, pol_out, back, xt, wide, gup = pl.pallas_call(
        kernel,
        out_shape=(
            jax.ShapeDtypeStruct((4, width), BF),
            jax.ShapeDtypeStruct((4, width), BF),
            jax.ShapeDtypeStruct((256, 256), BF),
            jax.ShapeDtypeStruct((256, width), BF),
            jax.ShapeDtypeStruct((256, 256), BF),
            jax.ShapeDtypeStruct((256, 256), BF),
        ),
        in_specs=[vmem] * 3 + [hbm] * 5,
        out_specs=(vmem, vmem, vmem, hbm, hbm, hbm),
        scratch_shapes=scratch,
        compiler_params=pltpu.CompilerParams(
            collective_id=0, has_side_effects=True, vmem_limit_bytes=56 * 2**20
        ),
        name="layer",
    )(
        token_adapter_index.reshape(1, -1),
        tokens,
        cotangent,
        gate,
        up,
        down,
        imaps.reshape(adapters * rank, width),
        omaps.reshape(adapters * rank, hidden),
    )
    ref_out, pol_out, in_grad, out_grad = pl.pallas_call(
        gradients,
        out_shape=(
            jax.ShapeDtypeStruct((4, width), BF),
            jax.ShapeDtypeStruct((4, width), BF),
            jax.ShapeDtypeStruct((adapters * rank, width), F32),
            jax.ShapeDtypeStruct((adapters * rank, hidden), F32),
        ),
        in_specs=[hbm] * 6,
        out_specs=(hbm,) * 4,
        scratch_shapes=[
            v((4, width), BF), v((4, width), BF), v((256, 256), BF), v((256, 256), BF), v((256, 256), BF),
            v((4, 256, 512), BF), v((4, 256, 512), F32), v((256, 256), F32),
            pltpu.SemaphoreType.DMA((9,)), pltpu.SemaphoreType.DMA((7,)),
        ],
        compiler_params=pltpu.CompilerParams(vmem_limit_bytes=60 * 2**20),
        name="gradients",
    )(ref_out, pol_out, back, wide, gup, xt)
    return (
        ref_out,
        pol_out,
        in_grad.reshape(adapters, rank, width),
        out_grad.reshape(adapters, rank, hidden),
    )


def solution(mesh):
    in_specs = (
        P("fsdp", "tp"),
        P(),
        P("tp", "fsdp"),
        P("tp", "fsdp"),
        P("fsdp", "tp"),
        P(None, None, "tp"),
        P(None, None, "fsdp"),
        P("fsdp", "tp"),
    )
    out_specs = (P("fsdp", "tp"), P("fsdp", "tp"), P(None, None, "tp"), P(None, None, "fsdp"))
    return jax.shard_map(body, mesh=mesh, in_specs=in_specs, out_specs=out_specs, check_vma=False)
```

```python
import functools

import jax
import jax.numpy as jnp
from jax import lax
from jax.experimental import pallas as pl
from jax.experimental.pallas import tpu as pltpu
from jax.sharding import PartitionSpec as P

MESH = pl.DeviceIdType.MESH
BF = jnp.bfloat16
F32 = jnp.float32

GROUPS = (("z", 0, 1024), ("p", 1024, 512), ("p", 1536, 512))


Z_STEPS = (4, 3, 5, 2, 6, 1, 7)
P_STEPS = (5, 3, 7, 1, 4, 2, 6)


def nt(a, b):
    return lax.dot_general(a, b, (((1,), (1,)), ((), ())), preferred_element_type=F32)


def tn(a, b):
    return lax.dot_general(a, b, (((0,), (0,)), ((), ())), preferred_element_type=F32)


def nn(a, b):
    return jnp.dot(a, b, preferred_element_type=F32)


def iota2(n, m):
    return (
        lax.broadcasted_iota(jnp.int32, (n, m), 0),
        lax.broadcasted_iota(jnp.int32, (n, m), 1),
    )


def as_matrix(condition):
    return condition.astype(F32).astype(BF)


def kernel(
    idx, tok, cot, gate, up, down, imaps, omaps,
    ref_out, pol_out, back_out, xt_out, wide_out, gup_out,
    gate_v, up_v, down_v, imaps_v, omaps_v,
    ta, tb, ca, cb, xt, ct,
    f1, s1, r1, s2, r2, e1, er1,
    f2, g1, gr1, g2, gr2, e2, er2,
    act_v, mask_v, lw_v, href, hpol, gup, hrp, hpp,
    ar0, ar1, ar1s, ar2, ar2s, ar3,
    *rest,
):
    ngroups = len(GROUPS)
    ysend, yrecv, zsend, zrecv = (rest[i * ngroups : (i + 1) * ngroups] for i in range(4))
    relay3, relay4, acc, wsem, ssem, rsem, osem = rest[4 * ngroups :]

    f = lax.axis_index("fsdp")
    t = lax.axis_index("tp")
    z, p, x, h, c = f // 8, f % 8, (f // 2) % 4, f % 2, t % 2

    def zdev(k):
        return {"fsdp": lax.rem(z + k + 8, 8) * 8 + p, "tp": t}

    def pidx(k):
        return lax.rem(x + k // 2, 4) * 2 + (h + k % 2) % 2

    def pdev(k):
        return {"fsdp": z * 8 + pidx(k), "tp": t}

    def tdev(k):
        return {"fsdp": f, "tp": ((t // 2 + k // 2) % 2) * 2 + (c + k % 2) % 2}

    counter = [0]
    pending = []

    def send(src, dst, device):
        n = counter[0]
        counter[0] += 1
        copy = pltpu.make_async_remote_copy(
            src_ref=src, dst_ref=dst, send_sem=ssem.at[n], recv_sem=rsem.at[n],
            device_id=device, device_id_type=MESH,
        )
        copy.start()
        pending.append(copy)
        return copy

    loads = []
    for n, (src, dst) in enumerate(
        ((gate, gate_v), (up, up_v), (imaps, imaps_v), (omaps, omaps_v), (down, down_v))
    ):
        load = pltpu.make_async_copy(src, dst, wsem.at[n])
        load.start()
        loads.append(load)

    barrier = pltpu.get_barrier_semaphore()
    partners = [zdev(k) for k in Z_STEPS] + [pdev(k) for k in P_STEPS] + [tdev(k) for k in range(1, 4)]
    for device in partners:
        pl.semaphore_signal(barrier, 1, device_id=device, device_id_type=MESH)

    i16, j4 = iota2(16, 4)
    for src, half_a, half_b in ((tok, ta, tb), (cot, ca, cb)):
        packed = None
        for q in range(4):
            spread = as_matrix(i16 == q * 4 + j4)
            term = nn(spread, src[:, q * 512 : (q + 1) * 512])
            packed = term if packed is None else packed + term
        packed = packed.astype(BF)
        half_a[z, p] = packed[:, :256]
        half_b[z, p] = packed[:, 256:]

    i8, j8 = iota2(8, 256)
    i256, j256 = iota2(256, 256)
    chosen = as_matrix(idx[...] == i8)
    order = as_matrix(j256 == ((i256 // 2) % 64) * 4 + (i256 // 128) * 2 + i256 % 2)
    mask_v[...] = nn(order, tn(chosen, as_matrix(i8 == j8 // 64)).astype(BF)).astype(BF)

    pl.semaphore_wait(barrier, len(partners))

    def first_hops(half_a, half_b):
        a = [send(half_a.at[z, p], half_a.at[z, p], pdev(k)) for k in P_STEPS]
        b = [send(half_b.at[z, p], half_b.at[z, p], zdev(k)) for k in Z_STEPS]
        return a, b

    def near_hops(half_a):
        return [send(half_a.at[z], half_a.at[z], zdev(k)) for k in (2, -2, 1, -1)]

    def plane_hops(half_b):
        return [send(half_b.at[:, p], half_b.at[:, p], pdev(k)) for k in P_STEPS]

    def far_hops(half_a, near):
        far = []
        for n, sign in ((0, 1), (1, -1)):
            near[n].wait_recv()
            block = lax.rem(z - 2 * sign + 8, 8)
            part = half_a.at[block, pl.ds(0 if sign == 1 else 4, 4)]
            far.append(send(part, part, zdev(2 * sign)))
            far.append(send(half_a.at[block], half_a.at[block], zdev(sign)))
        return far

    def arrived(copies):
        for copy in copies:
            copy.wait_recv()

    first_t = first_hops(ta, tb)
    first_c = first_hops(ca, cb)
    arrived(first_t[0])
    near_t = near_hops(ta)
    arrived(first_t[1])
    plane_t = plane_hops(tb)

    spread16 = as_matrix(
        j256 == ((i256 // 2) % 16) * 16 + (i256 // 64) * 4 + ((i256 // 32) % 2) * 2 + i256 % 2
    )
    i128, j128 = iota2(128, 128)
    plane_major = as_matrix(j128 == ((i128 // 2) % 8) * 16 + (i128 // 16) * 2 + i128 % 2)
    ifold, jfold = iota2(256, 128)
    fold_lo = as_matrix(ifold % 64 == jfold)
    fold_hi = as_matrix(ifold % 64 + 64 == jfold)
    regroup = as_matrix(
        j128
        == ((i128 // 4) % 2) * 64 + ((i128 // 8) % 2) * 32 + ((i128 // 2) % 2) * 16 + (i128 // 16) * 2 + i128 % 2
    )

    far_t = far_hops(ta, near_t)
    arrived(first_c[0])
    near_c = near_hops(ca)
    arrived(first_c[1])
    plane_c = plane_hops(cb)

    def unpack(half, n, whole):
        for g in range(4):
            block = nn(spread16, half[2 * g : 2 * g + 2].reshape(256, 256)).astype(BF)
            for q in range(4):
                for j in range(2):
                    whole[j * 128 + g * 32 : j * 128 + (g + 1) * 32, q * 512 + n * 256 : q * 512 + (n + 1) * 256] = (
                        block[q * 64 + j * 32 : q * 64 + (j + 1) * 32]
                    )

    rows = [slice(j * 128, (j + 1) * 128) for j in range(2)]
    own = [pl.ds(pl.multiple_of(j * 128 + c * 64, 64), 64) for j in range(2)]
    other = [pl.ds(pl.multiple_of(j * 128 + (1 - c) * 64, 64), 64) for j in range(2)]

    def to_line(j, copy):
        copy.wait_recv()
        s2[j] = (f1[own[j], :] + r1[j].astype(F32)).astype(BF)
        return send(s2.at[j], r2.at[j], tdev(2))

    arrived(plane_t)
    unpack(tb, 1, xt)
    for load in loads[:3]:
        load.wait()
    arrived(near_t[2:] + far_t)
    unpack(ta, 0, xt)
    f1[:, 0:256] = nn(xt[...], gate_v[...])
    f1[:, 256:512] = nn(xt[...], up_v[...])
    low = (nt(xt[...], imaps_v[...]) * mask_v[...].astype(F32)).astype(BF)
    f1[:, 512:640] = nn(low, fold_lo)
    core_t = []
    for j in range(2):
        s1[j] = f1[other[j], :].astype(BF)
        core_t.append(send(s1.at[j], r1.at[j], tdev(1)))
    xt_copy = pltpu.make_async_copy(xt, xt_out, osem.at[0])
    xt_copy.start()
    line_0 = to_line(0, core_t[0])
    line_1 = to_line(1, core_t[1])
    far_c = far_hops(ca, near_c)

    for load in loads[3:]:
        load.wait()

    def activate(j, copy):
        copy.wait_recv()
        total = s2[j].astype(F32) + r2[j].astype(F32)
        gate_values = total[:, 0:256]
        up_values = total[:, 256:512]
        lora_in = total[:, 512:640].astype(BF)
        wide = (nt(lora_in, fold_lo) * mask_v[own[j], :].astype(F32)).astype(BF)
        activated = gate_values / (1.0 + jnp.exp(-gate_values))
        act_v[j] = activated
        up_policy = up_values + nn(wide, omaps_v[...])
        e1[j, :, 0:256] = (activated * up_values).astype(BF)
        e1[j, :, 256:512] = (activated * up_policy).astype(BF)
        e1[j, :, 512:640] = lora_in
        pair = send(e1.at[j], er1.at[j], tdev(1))
        href[own[j], :] = e1[j, :, 0:256]
        hpol[own[j], :] = e1[j, :, 256:512]
        lw_v[own[j], :] = wide
        return pair

    def collect(j, copy):
        copy.wait_recv()
        href[other[j], :] = er1[j, :, 0:256]
        hpol[other[j], :] = er1[j, :, 256:512]
        lw_v[other[j], :] = (nt(er1[j, :, 512:640], fold_lo) * mask_v[other[j], :].astype(F32)).astype(BF)
        hrp[rows[j], :] = nn(plane_major, href[rows[j], :]).astype(BF)
        hpp[rows[j], :] = nn(plane_major, hpol[rows[j], :]).astype(BF)

    stage1 = [[[], []] for _ in GROUPS]

    def first_stage(n, j):
        kind, start, width = GROUPS[n]
        pair = (href, hpol) if kind == "z" else (hrp, hpp)
        half = width // 2
        for o in range(2):
            for q in range(2):
                block = nn(pair[o][rows[j], :], down_v[:, start + q * half : start + (q + 1) * half]).astype(BF)
                ysend[n][j, :, o, :, q * half : (q + 1) * half] = block.reshape(8, 16, half)
        copies = stage1[n][j]
        if kind == "z":
            for m, sign in ((0, 1), (1, -1)):
                copies.append(send(ysend[n].at[j, lax.rem(z + 3 * sign + 8, 8)], relay3.at[j, m], zdev(sign)))
                copies.append(send(ysend[n].at[j, lax.rem(z + 4, 8), m], relay4.at[j, m], zdev(2 * sign)))
            for m, sign in ((0, 1), (1, -1)):
                copies.append(send(ysend[n].at[j, lax.rem(z + sign + 8, 8)], yrecv[n].at[j, m], zdev(sign)))
        else:
            for k in P_STEPS:
                copies.append(send(ysend[n].at[j, pidx(k)], yrecv[n].at[j, p], pdev(k)))
            yrecv[n][j, p] = ysend[n][j, p]

    def relay(j):
        arrived(stage1[0][j][:4])
        for m, sign in ((0, 1), (1, -1)):
            block = ysend[0][j, lax.rem(z + 2 * sign + 8, 8)].astype(F32) + relay3[j, m].astype(F32)
            acc[j, m, m] = (block[m] + relay4[j, m].astype(F32)).astype(BF)
            acc[j, m, 1 - m] = block[1 - m].astype(BF)
            stage1[0][j].append(send(acc.at[j, m], yrecv[0].at[j, 2 + m], zdev(2 * sign)))

    pair_0 = activate(0, line_0)
    pair_1 = activate(1, line_1)
    arrived(near_c[2:] + plane_c + far_c)
    unpack(ca, 0, ct)
    unpack(cb, 1, ct)
    f2[...] = nt(ct[...], down_v[...])
    for j in range(2):
        g1[j] = f2[other[j], :].astype(BF)
    core_c = send(g1, gr1, tdev(1))
    collect(0, pair_0)
    first_stage(0, 0)
    core_c.wait_recv()
    for j in range(2):
        g2[j] = (f2[own[j], :] + gr1[j].astype(F32)).astype(BF)
    line_c = send(g2, gr2, tdev(2))
    first_stage(1, 0)
    collect(1, pair_1)
    first_stage(0, 1)
    relay(0)
    first_stage(1, 1)
    line_c.wait_recv()
    e2[...] = ((g2[...].astype(F32) + gr2[...].astype(F32)) * act_v[...]).astype(BF)
    mine = pl.ds(pl.multiple_of(t * 64, 64), 64)
    back = (nt(e2[t // 2], omaps_v[...]) * mask_v[mine, :].astype(F32)).astype(BF)
    ar0[...] = (nn(back[:32], fold_lo) + nn(back[32:], fold_hi)).astype(BF)
    sum1 = [send(ar0, ar1.at[p], pdev(k)) for k in P_STEPS]
    pair_c = send(e2, er2, tdev(1))
    ar1[p] = ar0[...]
    first_stage(2, 0)
    first_stage(2, 1)
    relay(1)

    stage2 = []

    def second_stage(n):
        kind, start, width = GROUPS[n]
        half = width // 2
        for j in range(2):
            arrived(stage1[n][j][4:] if kind == "z" else stage1[n][j])
        pieces = []
        for q in range(2):
            for o in range(2):
                columns = slice(q * half, (q + 1) * half)
                for j in range(2):
                    piece = jnp.sum(yrecv[n][j, :, o, :, columns].astype(F32), axis=0)
                    if kind == "z":
                        piece = piece + ysend[n][j, z, o, :, columns].astype(F32)
                    pieces.append(piece.astype(BF))
        stacked = jnp.concatenate(pieces, axis=0)
        zsend[n][...] = nn(regroup, stacked).astype(BF).reshape(8, 16, half)
        me = p if kind == "z" else z
        copies = []
        for k in P_STEPS if kind == "z" else Z_STEPS:
            to = pidx(k) if kind == "z" else lax.rem(z + k, 8)
            copies.append(
                send(zsend[n].at[to], zrecv[n].at[me], pdev(k) if kind == "z" else zdev(k))
            )
        zrecv[n][me] = zsend[n][me]
        stage2.append(copies)

    for copy in sum1:
        copy.wait_recv()
    ar1s[...] = jnp.sum(ar1[...].astype(F32), axis=0).astype(BF)
    ar2[z] = ar1s[...]
    sum2 = [send(ar1s, ar2.at[z], zdev(k)) for k in Z_STEPS]
    second_stage(0)
    second_stage(1)
    for j in range(2):
        gup[own[j], :] = e2[j]
    pair_c.wait_recv()
    for j in range(2):
        gup[other[j], :] = er2[j]
    wide_copy = pltpu.make_async_copy(lw_v, wide_out, osem.at[1])
    wide_copy.start()
    gup_copy = pltpu.make_async_copy(gup, gup_out, osem.at[2])
    gup_copy.start()
    second_stage(2)
    for copy in sum2:
        copy.wait_recv()
    ar2s[...] = jnp.sum(ar2[...].astype(F32), axis=0).astype(BF)
    ar3[t] = ar2s[...]
    sum3 = [send(ar2s, ar3.at[t], tdev(k)) for k in range(1, 4)]
    for copy in sum3:
        copy.wait_recv()
    wides = []
    for k in range(4):
        for fold in (fold_lo, fold_hi):
            wides.append(nt(ar3[k], fold))
    back_out[...] = (jnp.concatenate(wides, axis=0) * mask_v[...].astype(F32)).astype(BF)

    i4, j16 = iota2(4, 16)
    for n, (kind, start, width) in enumerate(GROUPS):
        half = width // 2
        for copy in stage2[n]:
            copy.wait_recv()
        total = jnp.sum(zrecv[n][...].astype(F32), axis=0).astype(BF)
        for o, out in enumerate((ref_out, pol_out)):
            for q in range(2):
                pick = as_matrix(j16 == o * 8 + q * 4 + i4)
                out[:, start + q * half : start + (q + 1) * half] = nn(pick, total).astype(BF)

    for copy in (xt_copy, wide_copy, gup_copy):
        copy.wait()
    for copy in pending:
        copy.wait_send()


def gradients(
    ref_in, pol_in, back, wide, gup, xt, ref_out, pol_out, in_grad, out_grad,
    rv, pv, bv, wv, uv, xv, gv, ov, isem, osem,
):
    sources = [back, wide, gup, ref_in, pol_in] + [xt.at[:, pl.ds(k * 512, 512)] for k in range(4)]
    places = [bv, wv, uv, rv, pv] + [xv.at[k] for k in range(4)]
    loads = {}
    for n in (0, 5, 6, 7, 8, 3, 4, 1, 2):
        load = pltpu.make_async_copy(sources[n], places[n], isem.at[n])
        load.start()
        loads[n] = load
    stores = []

    def store(src, dst):
        copy = pltpu.make_async_copy(src, dst, osem.at[len(stores)])
        copy.start()
        stores.append(copy)

    loads[0].wait()
    for k in range(4):
        loads[5 + k].wait()
        gv[k] = tn(bv[...], xv[k])
        store(gv.at[k], in_grad.at[:, pl.ds(k * 512, 512)])
    for n in (1, 2, 3, 4):
        loads[n].wait()
    store(rv, ref_out)
    store(pv, pol_out)
    ov[...] = tn(wv[...], uv[...])
    store(ov, out_grad)
    for copy in stores:
        copy.wait()


COPIES = 2 * (14 + 11 + 4) + 6 + 3 + 16 + 28 + 21 + 17


def body(tokens, token_adapter_index, gate, up, down, imaps, omaps, cotangent):
    adapters, rank, width = imaps.shape
    hidden = omaps.shape[2]
    vmem = pl.BlockSpec(memory_space=pltpu.VMEM)
    hbm = pl.BlockSpec(memory_space=pl.ANY)
    v = pltpu.VMEM
    scratch = [
        v((2048, 256), BF), v((2048, 256), BF), v((256, 2048), BF), v((256, 2048), BF), v((256, 256), BF),
        v((8, 8, 16, 256), BF), v((8, 8, 16, 256), BF), v((8, 8, 16, 256), BF), v((8, 8, 16, 256), BF),
        v((256, 2048), BF), v((256, 2048), BF),
        v((256, 640), F32), v((2, 64, 640), BF), v((2, 64, 640), BF), v((2, 64, 640), BF), v((2, 64, 640), BF),
        v((2, 64, 640), BF), v((2, 64, 640), BF),
        v((256, 256), F32), v((2, 64, 256), BF), v((2, 64, 256), BF), v((2, 64, 256), BF), v((2, 64, 256), BF),
        v((2, 64, 256), BF), v((2, 64, 256), BF),
        v((2, 64, 256), F32), v((256, 256), BF), v((256, 256), BF), v((256, 256), BF), v((256, 256), BF),
        v((256, 256), BF), v((256, 256), BF), v((256, 256), BF),
        v((32, 128), BF), v((8, 32, 128), BF), v((32, 128), BF), v((8, 32, 128), BF), v((32, 128), BF),
        v((4, 32, 128), BF),
    ]
    scratch += [v((2, 8, 2, 16, w), BF) for _, _, w in GROUPS]
    scratch += [v((2, 4 if kind == "z" else 8, 2, 16, w), BF) for kind, _, w in GROUPS]
    scratch += [v((8, 16, w // 2), BF) for _, _, w in GROUPS] * 2
    first = GROUPS[0][2]
    scratch += [v((2, 2, 2, 16, first), BF), v((2, 2, 16, first), BF), v((2, 2, 2, 16, first), BF)]
    scratch += [
        pltpu.SemaphoreType.DMA((5,)),
        pltpu.SemaphoreType.DMA((COPIES,)),
        pltpu.SemaphoreType.DMA((COPIES,)),
        pltpu.SemaphoreType.DMA((3,)),
    ]
    ref_out, pol_out, back, xt, wide, gup = pl.pallas_call(
        kernel,
        out_shape=(
            jax.ShapeDtypeStruct((4, width), BF),
            jax.ShapeDtypeStruct((4, width), BF),
            jax.ShapeDtypeStruct((256, 256), BF),
            jax.ShapeDtypeStruct((256, width), BF),
            jax.ShapeDtypeStruct((256, 256), BF),
            jax.ShapeDtypeStruct((256, 256), BF),
        ),
        in_specs=[vmem] * 3 + [hbm] * 5,
        out_specs=(vmem, vmem, vmem, hbm, hbm, hbm),
        scratch_shapes=scratch,
        compiler_params=pltpu.CompilerParams(
            collective_id=0, has_side_effects=True, vmem_limit_bytes=56 * 2**20
        ),
        name="layer",
    )(
        token_adapter_index.reshape(1, -1),
        tokens,
        cotangent,
        gate,
        up,
        down,
        imaps.reshape(adapters * rank, width),
        omaps.reshape(adapters * rank, hidden),
    )
    ref_out, pol_out, in_grad, out_grad = pl.pallas_call(
        gradients,
        out_shape=(
            jax.ShapeDtypeStruct((4, width), BF),
            jax.ShapeDtypeStruct((4, width), BF),
            jax.ShapeDtypeStruct((adapters * rank, width), F32),
            jax.ShapeDtypeStruct((adapters * rank, hidden), F32),
        ),
        in_specs=[hbm] * 6,
        out_specs=(hbm,) * 4,
        scratch_shapes=[
            v((4, width), BF), v((4, width), BF), v((256, 256), BF), v((256, 256), BF), v((256, 256), BF),
            v((4, 256, 512), BF), v((4, 256, 512), F32), v((256, 256), F32),
            pltpu.SemaphoreType.DMA((9,)), pltpu.SemaphoreType.DMA((7,)),
        ],
        compiler_params=pltpu.CompilerParams(vmem_limit_bytes=60 * 2**20),
        name="gradients",
    )(ref_out, pol_out, back, wide, gup, xt)
    return (
        ref_out,
        pol_out,
        in_grad.reshape(adapters, rank, width),
        out_grad.reshape(adapters, rank, hidden),
    )


def solution(mesh):
    in_specs = (
        P("fsdp", "tp"),
        P(),
        P("tp", "fsdp"),
        P("tp", "fsdp"),
        P("fsdp", "tp"),
        P(None, None, "tp"),
        P(None, None, "fsdp"),
        P("fsdp", "tp"),
    )
    out_specs = (P("fsdp", "tp"), P("fsdp", "tp"), P(None, None, "tp"), P(None, None, "fsdp"))
    return jax.shard_map(body, mesh=mesh, in_specs=in_specs, out_specs=out_specs, check_vma=False)
```

```python
import functools

import jax
import jax.numpy as jnp
from jax import lax
from jax.experimental import pallas as pl
from jax.experimental.pallas import tpu as pltpu
from jax.sharding import PartitionSpec as P

MESH = pl.DeviceIdType.MESH
BF = jnp.bfloat16
F32 = jnp.float32

GROUPS = (("z", 0, 1024), ("p", 1024, 512), ("p", 1536, 512))


Z_STEPS = (4, 3, 5, 2, 6, 1, 7)
P_STEPS = (5, 3, 7, 1, 4, 2, 6)


def nt(a, b):
    return lax.dot_general(a, b, (((1,), (1,)), ((), ())), preferred_element_type=F32)


def tn(a, b):
    return lax.dot_general(a, b, (((0,), (0,)), ((), ())), preferred_element_type=F32)


def nn(a, b):
    return jnp.dot(a, b, preferred_element_type=F32)


def iota2(n, m):
    return (
        lax.broadcasted_iota(jnp.int32, (n, m), 0),
        lax.broadcasted_iota(jnp.int32, (n, m), 1),
    )


def as_matrix(condition):
    return condition.astype(F32).astype(BF)


def kernel(
    idx, tok, cot, gate, up, down, imaps, omaps,
    ref_out, pol_out, back_out, xt_out, wide_out, gup_out,
    gate_v, up_v, down_v, imaps_v, omaps_v,
    ta, tb, ca, cb, xt, ct,
    f1, s1, r1, s2, r2, e1, er1,
    f2, g1, gr1, g2, gr2, e2, er2,
    act_v, mask_v, lw_v, href, hpol, gup, hrp, hpp,
    ar0, ar1, ar1s, ar2, ar2s, ar3,
    *rest,
):
    ngroups = len(GROUPS)
    ysend, yrecv, zsend, zrecv = (rest[i * ngroups : (i + 1) * ngroups] for i in range(4))
    relay3, relay4, acc, wsem, ssem, rsem, osem = rest[4 * ngroups :]

    f = lax.axis_index("fsdp")
    t = lax.axis_index("tp")
    z, p, x, h, c = f // 8, f % 8, (f // 2) % 4, f % 2, t % 2

    def zdev(k):
        return {"fsdp": lax.rem(z + k + 8, 8) * 8 + p, "tp": t}

    def pidx(k):
        return lax.rem(x + k // 2, 4) * 2 + (h + k % 2) % 2

    def pdev(k):
        return {"fsdp": z * 8 + pidx(k), "tp": t}

    def tdev(k):
        return {"fsdp": f, "tp": ((t // 2 + k // 2) % 2) * 2 + (c + k % 2) % 2}

    counter = [0]
    pending = []

    def send(src, dst, device):
        n = counter[0]
        counter[0] += 1
        copy = pltpu.make_async_remote_copy(
            src_ref=src, dst_ref=dst, send_sem=ssem.at[n], recv_sem=rsem.at[n],
            device_id=device, device_id_type=MESH,
        )
        copy.start()
        pending.append(copy)
        return copy

    loads = []
    for n, (src, dst) in enumerate(
        ((gate, gate_v), (up, up_v), (imaps, imaps_v), (omaps, omaps_v), (down, down_v))
    ):
        load = pltpu.make_async_copy(src, dst, wsem.at[n])
        load.start()
        loads.append(load)

    barrier = pltpu.get_barrier_semaphore()
    partners = [zdev(k) for k in Z_STEPS] + [pdev(k) for k in P_STEPS] + [tdev(k) for k in range(1, 4)]
    for device in partners:
        pl.semaphore_signal(barrier, 1, device_id=device, device_id_type=MESH)

    i16, j4 = iota2(16, 4)
    for src, half_a, half_b in ((tok, ta, tb), (cot, ca, cb)):
        packed = None
        for q in range(4):
            spread = as_matrix(i16 == q * 4 + j4)
            term = nn(spread, src[:, q * 512 : (q + 1) * 512])
            packed = term if packed is None else packed + term
        packed = packed.astype(BF)
        half_a[z, p] = packed[:, :256]
        half_b[z, p] = packed[:, 256:]

    i8, j8 = iota2(8, 256)
    i256, j256 = iota2(256, 256)
    chosen = as_matrix(idx[...] == i8)
    order = as_matrix(j256 == ((i256 // 2) % 64) * 4 + (i256 // 128) * 2 + i256 % 2)
    mask_v[...] = nn(order, tn(chosen, as_matrix(i8 == j8 // 64)).astype(BF)).astype(BF)

    pl.semaphore_wait(barrier, len(partners))

    def first_hops(half_a, half_b):
        a = [send(half_a.at[z, p], half_a.at[z, p], pdev(k)) for k in P_STEPS]
        b = [send(half_b.at[z, p], half_b.at[z, p], zdev(k)) for k in Z_STEPS]
        return a, b

    def near_hops(half_a):
        return [send(half_a.at[z], half_a.at[z], zdev(k)) for k in (2, -2, 1, -1)]

    def plane_hops(half_b):
        return [send(half_b.at[:, p], half_b.at[:, p], pdev(k)) for k in P_STEPS]

    def far_hops(half_a, near):
        far = []
        for n, sign in ((0, 1), (1, -1)):
            near[n].wait_recv()
            block = lax.rem(z - 2 * sign + 8, 8)
            part = half_a.at[block, pl.ds(0 if sign == 1 else 4, 4)]
            far.append(send(part, part, zdev(2 * sign)))
            far.append(send(half_a.at[block], half_a.at[block], zdev(sign)))
        return far

    def arrived(copies):
        for copy in copies:
            copy.wait_recv()

    first_t = first_hops(ta, tb)
    first_c = first_hops(ca, cb)
    arrived(first_t[0])
    near_t = near_hops(ta)
    arrived(first_t[1])
    plane_t = plane_hops(tb)

    spread16 = as_matrix(
        j256 == ((i256 // 2) % 16) * 16 + (i256 // 64) * 4 + ((i256 // 32) % 2) * 2 + i256 % 2
    )
    i128, j128 = iota2(128, 128)
    plane_major = as_matrix(j128 == ((i128 // 2) % 8) * 16 + (i128 // 16) * 2 + i128 % 2)
    ifold, jfold = iota2(256, 128)
    fold_lo = as_matrix(ifold % 64 == jfold)
    fold_hi = as_matrix(ifold % 64 + 64 == jfold)
    regroup = as_matrix(
        j128
        == ((i128 // 4) % 2) * 64 + ((i128 // 8) % 2) * 32 + ((i128 // 2) % 2) * 16 + (i128 // 16) * 2 + i128 % 2
    )

    far_t = far_hops(ta, near_t)
    arrived(first_c[0])
    near_c = near_hops(ca)
    arrived(first_c[1])
    plane_c = plane_hops(cb)

    def unpack(half, n, whole):
        for g in range(4):
            block = nn(spread16, half[2 * g : 2 * g + 2].reshape(256, 256)).astype(BF)
            for q in range(4):
                for j in range(2):
                    whole[j * 128 + g * 32 : j * 128 + (g + 1) * 32, q * 512 + n * 256 : q * 512 + (n + 1) * 256] = (
                        block[q * 64 + j * 32 : q * 64 + (j + 1) * 32]
                    )

    rows = [slice(j * 128, (j + 1) * 128) for j in range(2)]
    own = [pl.ds(pl.multiple_of(j * 128 + c * 64, 64), 64) for j in range(2)]
    other = [pl.ds(pl.multiple_of(j * 128 + (1 - c) * 64, 64), 64) for j in range(2)]

    def to_line(j, copy):
        copy.wait_recv()
        s2[j] = (f1[own[j], :] + r1[j].astype(F32)).astype(BF)
        return send(s2.at[j], r2.at[j], tdev(2))

    arrived(plane_t)
    unpack(tb, 1, xt)
    for load in loads[:3]:
        load.wait()
    arrived(near_t[2:] + far_t)
    unpack(ta, 0, xt)
    f1[:, 0:256] = nn(xt[...], gate_v[...])
    f1[:, 256:512] = nn(xt[...], up_v[...])
    low = (nt(xt[...], imaps_v[...]) * mask_v[...].astype(F32)).astype(BF)
    f1[:, 512:640] = nn(low, fold_lo)
    core_t = []
    for j in range(2):
        s1[j] = f1[other[j], :].astype(BF)
        core_t.append(send(s1.at[j], r1.at[j], tdev(1)))
    line_0 = to_line(0, core_t[0])
    line_1 = to_line(1, core_t[1])
    far_c = far_hops(ca, near_c)

    for load in loads[3:]:
        load.wait()

    def activate(j, copy):
        copy.wait_recv()
        total = s2[j].astype(F32) + r2[j].astype(F32)
        gate_values = total[:, 0:256]
        up_values = total[:, 256:512]
        lora_in = total[:, 512:640].astype(BF)
        wide = (nt(lora_in, fold_lo) * mask_v[own[j], :].astype(F32)).astype(BF)
        activated = gate_values / (1.0 + jnp.exp(-gate_values))
        act_v[j] = activated
        up_policy = up_values + nn(wide, omaps_v[...])
        e1[j, :, 0:256] = (activated * up_values).astype(BF)
        e1[j, :, 256:512] = (activated * up_policy).astype(BF)
        e1[j, :, 512:640] = lora_in
        pair = send(e1.at[j], er1.at[j], tdev(1))
        href[own[j], :] = e1[j, :, 0:256]
        hpol[own[j], :] = e1[j, :, 256:512]
        lw_v[own[j], :] = wide
        return pair

    def collect(j, copy):
        copy.wait_recv()
        href[other[j], :] = er1[j, :, 0:256]
        hpol[other[j], :] = er1[j, :, 256:512]
        lw_v[other[j], :] = (nt(er1[j, :, 512:640], fold_lo) * mask_v[other[j], :].astype(F32)).astype(BF)
        hrp[rows[j], :] = nn(plane_major, href[rows[j], :]).astype(BF)
        hpp[rows[j], :] = nn(plane_major, hpol[rows[j], :]).astype(BF)

    stage1 = [[[], []] for _ in GROUPS]

    def first_stage(n, j):
        kind, start, width = GROUPS[n]
        pair = (href, hpol) if kind == "z" else (hrp, hpp)
        half = width // 2
        for o in range(2):
            for q in range(2):
                block = nn(pair[o][rows[j], :], down_v[:, start + q * half : start + (q + 1) * half]).astype(BF)
                ysend[n][j, :, o, :, q * half : (q + 1) * half] = block.reshape(8, 16, half)
        copies = stage1[n][j]
        if kind == "z":
            for m, sign in ((0, 1), (1, -1)):
                copies.append(send(ysend[n].at[j, lax.rem(z + 3 * sign + 8, 8)], relay3.at[j, m], zdev(sign)))
                copies.append(send(ysend[n].at[j, lax.rem(z + 4, 8), m], relay4.at[j, m], zdev(2 * sign)))
            for m, sign in ((0, 1), (1, -1)):
                copies.append(send(ysend[n].at[j, lax.rem(z + sign + 8, 8)], yrecv[n].at[j, m], zdev(sign)))
        else:
            for k in P_STEPS:
                copies.append(send(ysend[n].at[j, pidx(k)], yrecv[n].at[j, p], pdev(k)))
            yrecv[n][j, p] = ysend[n][j, p]

    def relay(j):
        arrived(stage1[0][j][:4])
        for m, sign in ((0, 1), (1, -1)):
            block = ysend[0][j, lax.rem(z + 2 * sign + 8, 8)].astype(F32) + relay3[j, m].astype(F32)
            acc[j, m, m] = (block[m] + relay4[j, m].astype(F32)).astype(BF)
            acc[j, m, 1 - m] = block[1 - m].astype(BF)
            stage1[0][j].append(send(acc.at[j, m], yrecv[0].at[j, 2 + m], zdev(2 * sign)))

    xt_copy = pltpu.make_async_copy(xt, xt_out, osem.at[0])
    xt_copy.start()
    pair_0 = activate(0, line_0)
    arrived(plane_c)
    unpack(cb, 1, ct)
    pair_1 = activate(1, line_1)
    arrived(near_c[2:] + far_c)
    unpack(ca, 0, ct)
    f2[...] = nt(ct[...], down_v[...])
    for j in range(2):
        g1[j] = f2[other[j], :].astype(BF)
    core_c = send(g1, gr1, tdev(1))
    collect(0, pair_0)
    first_stage(0, 0)
    core_c.wait_recv()
    for j in range(2):
        g2[j] = (f2[own[j], :] + gr1[j].astype(F32)).astype(BF)
    line_c = send(g2, gr2, tdev(2))
    first_stage(1, 0)
    collect(1, pair_1)
    first_stage(0, 1)
    relay(0)
    first_stage(1, 1)
    line_c.wait_recv()
    e2[...] = ((g2[...].astype(F32) + gr2[...].astype(F32)) * act_v[...]).astype(BF)
    mine = pl.ds(pl.multiple_of(t * 64, 64), 64)
    back = (nt(e2[t // 2], omaps_v[...]) * mask_v[mine, :].astype(F32)).astype(BF)
    ar0[...] = (nn(back[:32], fold_lo) + nn(back[32:], fold_hi)).astype(BF)
    sum1 = [send(ar0, ar1.at[p], pdev(k)) for k in P_STEPS]
    pair_c = send(e2, er2, tdev(1))
    ar1[p] = ar0[...]
    first_stage(2, 0)
    first_stage(2, 1)
    relay(1)

    stage2 = []

    def second_stage(n):
        kind, start, width = GROUPS[n]
        half = width // 2
        for j in range(2):
            arrived(stage1[n][j][4:] if kind == "z" else stage1[n][j])
        pieces = []
        for q in range(2):
            for o in range(2):
                columns = slice(q * half, (q + 1) * half)
                for j in range(2):
                    piece = jnp.sum(yrecv[n][j, :, o, :, columns].astype(F32), axis=0)
                    if kind == "z":
                        piece = piece + ysend[n][j, z, o, :, columns].astype(F32)
                    pieces.append(piece.astype(BF))
        stacked = jnp.concatenate(pieces, axis=0)
        zsend[n][...] = nn(regroup, stacked).astype(BF).reshape(8, 16, half)
        me = p if kind == "z" else z
        copies = []
        for k in P_STEPS if kind == "z" else Z_STEPS:
            to = pidx(k) if kind == "z" else lax.rem(z + k, 8)
            copies.append(
                send(zsend[n].at[to], zrecv[n].at[me], pdev(k) if kind == "z" else zdev(k))
            )
        zrecv[n][me] = zsend[n][me]
        stage2.append(copies)

    for copy in sum1:
        copy.wait_recv()
    ar1s[...] = jnp.sum(ar1[...].astype(F32), axis=0).astype(BF)
    ar2[z] = ar1s[...]
    sum2 = [send(ar1s, ar2.at[z], zdev(k)) for k in Z_STEPS]
    second_stage(0)
    second_stage(1)
    for j in range(2):
        gup[own[j], :] = e2[j]
    pair_c.wait_recv()
    for j in range(2):
        gup[other[j], :] = er2[j]
    wide_copy = pltpu.make_async_copy(lw_v, wide_out, osem.at[1])
    wide_copy.start()
    gup_copy = pltpu.make_async_copy(gup, gup_out, osem.at[2])
    gup_copy.start()
    second_stage(2)
    for copy in sum2:
        copy.wait_recv()
    ar2s[...] = jnp.sum(ar2[...].astype(F32), axis=0).astype(BF)
    ar3[t] = ar2s[...]
    sum3 = [send(ar2s, ar3.at[t], tdev(k)) for k in range(1, 4)]
    for copy in sum3:
        copy.wait_recv()
    wides = []
    for k in range(4):
        for fold in (fold_lo, fold_hi):
            wides.append(nt(ar3[k], fold))
    back_out[...] = (jnp.concatenate(wides, axis=0) * mask_v[...].astype(F32)).astype(BF)

    i4, j16 = iota2(4, 16)
    for n, (kind, start, width) in enumerate(GROUPS):
        half = width // 2
        for copy in stage2[n]:
            copy.wait_recv()
        total = jnp.sum(zrecv[n][...].astype(F32), axis=0).astype(BF)
        for o, out in enumerate((ref_out, pol_out)):
            for q in range(2):
                pick = as_matrix(j16 == o * 8 + q * 4 + i4)
                out[:, start + q * half : start + (q + 1) * half] = nn(pick, total).astype(BF)

    for copy in (xt_copy, wide_copy, gup_copy):
        copy.wait()
    for copy in pending:
        copy.wait_send()


def gradients(
    ref_in, pol_in, back, wide, gup, xt, ref_out, pol_out, in_grad, out_grad,
    rv, pv, bv, wv, uv, xv, gv, ov, isem, osem,
):
    sources = [back, wide, gup, ref_in, pol_in] + [xt.at[:, pl.ds(k * 512, 512)] for k in range(4)]
    places = [bv, wv, uv, rv, pv] + [xv.at[k] for k in range(4)]
    loads = {}
    for n in (0, 5, 6, 7, 8, 3, 4, 1, 2):
        load = pltpu.make_async_copy(sources[n], places[n], isem.at[n])
        load.start()
        loads[n] = load
    stores = []

    def store(src, dst):
        copy = pltpu.make_async_copy(src, dst, osem.at[len(stores)])
        copy.start()
        stores.append(copy)

    loads[0].wait()
    for k in range(4):
        loads[5 + k].wait()
        gv[k] = tn(bv[...], xv[k])
        store(gv.at[k], in_grad.at[:, pl.ds(k * 512, 512)])
    for n in (1, 2, 3, 4):
        loads[n].wait()
    store(rv, ref_out)
    store(pv, pol_out)
    ov[...] = tn(wv[...], uv[...])
    store(ov, out_grad)
    for copy in stores:
        copy.wait()


COPIES = 2 * (14 + 11 + 4) + 6 + 3 + 16 + 28 + 21 + 17


def body(tokens, token_adapter_index, gate, up, down, imaps, omaps, cotangent):
    adapters, rank, width = imaps.shape
    hidden = omaps.shape[2]
    vmem = pl.BlockSpec(memory_space=pltpu.VMEM)
    hbm = pl.BlockSpec(memory_space=pl.ANY)
    v = pltpu.VMEM
    scratch = [
        v((2048, 256), BF), v((2048, 256), BF), v((256, 2048), BF), v((256, 2048), BF), v((256, 256), BF),
        v((8, 8, 16, 256), BF), v((8, 8, 16, 256), BF), v((8, 8, 16, 256), BF), v((8, 8, 16, 256), BF),
        v((256, 2048), BF), v((256, 2048), BF),
        v((256, 640), F32), v((2, 64, 640), BF), v((2, 64, 640), BF), v((2, 64, 640), BF), v((2, 64, 640), BF),
        v((2, 64, 640), BF), v((2, 64, 640), BF),
        v((256, 256), F32), v((2, 64, 256), BF), v((2, 64, 256), BF), v((2, 64, 256), BF), v((2, 64, 256), BF),
        v((2, 64, 256), BF), v((2, 64, 256), BF),
        v((2, 64, 256), F32), v((256, 256), BF), v((256, 256), BF), v((256, 256), BF), v((256, 256), BF),
        v((256, 256), BF), v((256, 256), BF), v((256, 256), BF),
        v((32, 128), BF), v((8, 32, 128), BF), v((32, 128), BF), v((8, 32, 128), BF), v((32, 128), BF),
        v((4, 32, 128), BF),
    ]
    scratch += [v((2, 8, 2, 16, w), BF) for _, _, w in GROUPS]
    scratch += [v((2, 4 if kind == "z" else 8, 2, 16, w), BF) for kind, _, w in GROUPS]
    scratch += [v((8, 16, w // 2), BF) for _, _, w in GROUPS] * 2
    first = GROUPS[0][2]
    scratch += [v((2, 2, 2, 16, first), BF), v((2, 2, 16, first), BF), v((2, 2, 2, 16, first), BF)]
    scratch += [
        pltpu.SemaphoreType.DMA((5,)),
        pltpu.SemaphoreType.DMA((COPIES,)),
        pltpu.SemaphoreType.DMA((COPIES,)),
        pltpu.SemaphoreType.DMA((3,)),
    ]
    ref_out, pol_out, back, xt, wide, gup = pl.pallas_call(
        kernel,
        out_shape=(
            jax.ShapeDtypeStruct((4, width), BF),
            jax.ShapeDtypeStruct((4, width), BF),
            jax.ShapeDtypeStruct((256, 256), BF),
            jax.ShapeDtypeStruct((256, width), BF),
            jax.ShapeDtypeStruct((256, 256), BF),
            jax.ShapeDtypeStruct((256, 256), BF),
        ),
        in_specs=[vmem] * 3 + [hbm] * 5,
        out_specs=(vmem, vmem, vmem, hbm, hbm, hbm),
        scratch_shapes=scratch,
        compiler_params=pltpu.CompilerParams(
            collective_id=0, has_side_effects=True, vmem_limit_bytes=56 * 2**20
        ),
        name="layer",
    )(
        token_adapter_index.reshape(1, -1),
        tokens,
        cotangent,
        gate,
        up,
        down,
        imaps.reshape(adapters * rank, width),
        omaps.reshape(adapters * rank, hidden),
    )
    ref_out, pol_out, in_grad, out_grad = pl.pallas_call(
        gradients,
        out_shape=(
            jax.ShapeDtypeStruct((4, width), BF),
            jax.ShapeDtypeStruct((4, width), BF),
            jax.ShapeDtypeStruct((adapters * rank, width), F32),
            jax.ShapeDtypeStruct((adapters * rank, hidden), F32),
        ),
        in_specs=[hbm] * 6,
        out_specs=(hbm,) * 4,
        scratch_shapes=[
            v((4, width), BF), v((4, width), BF), v((256, 256), BF), v((256, 256), BF), v((256, 256), BF),
            v((4, 256, 512), BF), v((4, 256, 512), F32), v((256, 256), F32),
            pltpu.SemaphoreType.DMA((9,)), pltpu.SemaphoreType.DMA((7,)),
        ],
        compiler_params=pltpu.CompilerParams(vmem_limit_bytes=60 * 2**20),
        name="gradients",
    )(ref_out, pol_out, back, wide, gup, xt)
    return (
        ref_out,
        pol_out,
        in_grad.reshape(adapters, rank, width),
        out_grad.reshape(adapters, rank, hidden),
    )


def solution(mesh):
    in_specs = (
        P("fsdp", "tp"),
        P(),
        P("tp", "fsdp"),
        P("tp", "fsdp"),
        P("fsdp", "tp"),
        P(None, None, "tp"),
        P(None, None, "fsdp"),
        P("fsdp", "tp"),
    )
    out_specs = (P("fsdp", "tp"), P("fsdp", "tp"), P(None, None, "tp"), P(None, None, "fsdp"))
    return jax.shard_map(body, mesh=mesh, in_specs=in_specs, out_specs=out_specs, check_vma=False)
```
